32 devices in a mesh: dom: 8 (over z, x), inst: 4 (over y, core).
Axes of the slice: x: 2, y: 2, z: 4, core: 2. Of those that a mesh axis runs over, the one named last changes fastest.
Arguments:
- state: float32 [5, 16, 4096], P(None, 'inst', 'dom'), may hold values from -0.65 to 3.75, as said below
- cell_volume: float32 [4096], P('dom'), may hold values from 1 to 4
- step_size: float32 [4096], P('dom'), may hold values from 0.02 to 0.1
- face_normal: float32 [3, 16384], P(None, 'dom'), may hold values from -1 to 1
- owner_arm: float32 [3, 16384], P(None, 'dom'), may hold values from -0.09 to 0.09
- neighbor_arm: float32 [3, 16384], P(None, 'dom'), may hold values from -0.09 to 0.09
- face_owner: int32 [16384], P('dom'), may hold values from 0 to 511, as said below
- face_neighbor: int32 [16384], P('dom'), may hold values from 0 to 767, as said below
- face_count: int32 [8], P('dom'), may hold values from 1024 to 2048, as said below
- send_cells: int32 [32, 64], P('dom'), may hold values from 0 to 511
Outputs:
- new_state: float32 [5, 16, 4096], P(None, 'inst', 'dom')
- residual: float32 [5, 16, 4096], P(None, 'inst', 'dom')
The draws below stay inside these ranges and needn't reach their ends.
Inputs may be any that keep to these rules, and one draw needn't show every extreme that they name: The state is physical: density 0.7 to 1.3 and pressure 0.4 (E - |m|^2 / (2 rho)) 0.7 to 1.3. `face_owner`: local ids of cells of the face's own partition. `face_neighbor`: either a local cell id below 512, or the ghost id 512 + k * 64 + s of block k; blocks of partitions that do not exist are never named. `face_count`: live face slots come first in each partition; some partition has all 2048 slots live. `send_cells`: row 4 q + k lists cells of partition q that fill ghost block k of partition q - o_k, o = (-2, -1, 1, 2); slots that no face names are padding.
All inputs are finite; a program needn't handle non-finite values.
Results may differ from the reference program's by a relative error of at most 0.0003.
Values sent between devices are 32-bit elements; how exact they have to be, the bound alone decides.
A program may use at most 128 MiB of HBM per device.

```python
import math
import jax
import jax.numpy as jnp
from jax import lax

NVAR = 5
INST = 16
C_DEV = 512
SLOTS = 64
F_DEV = 2048
CELLS = 4096
FACES = 16384
LISTS = 32


HEAT_RATIO = 1.4


PEER_OFFSETS = (-2, -1, 1, 2)


def ghost_counts(key):
    partitions = FACES // F_DEV
    counts = jax.random.randint(jax.random.fold_in(key, 21), (partitions, 4), SLOTS // 2, SLOTS + 1)
    return counts.at[2, 3].set(SLOTS)


def draw_state(key, part):
    grid_shape = (INST, CELLS)
    subkeys = jax.random.split(jax.random.fold_in(key, 51), 3)
    density = jax.random.uniform(subkeys[0], grid_shape, jnp.float32, 0.85, 1.15)
    velocity = jnp.clip(0.25 * jax.random.normal(subkeys[1], (3,) + grid_shape, jnp.float32), -0.5, 0.5)
    pressure = jax.random.uniform(subkeys[2], grid_shape, jnp.float32, 0.85, 1.15)
    momentum = density * velocity
    energy = pressure / (HEAT_RATIO - 1.0) + 0.5 * density * jnp.sum(velocity * velocity, axis=0)
    return jnp.concatenate([density[None], momentum, energy[None]], axis=0).astype(jnp.float32)


def draw_face_owner(key, part):
    partitions = FACES // F_DEV
    owners = jax.random.randint(jax.random.fold_in(key, 11), (partitions, F_DEV), 0, C_DEV)
    owners = owners.at[0, 0].set(C_DEV - 1).at[0, 1].set(0)
    return owners.reshape(FACES).astype(jnp.int32)


def draw_face_neighbor(key, part):
    partitions = FACES // F_DEV
    counts = ghost_counts(key)
    owned_id = jax.random.randint(jax.random.fold_in(key, 31), (partitions, F_DEV), 0, C_DEV)
    choose = jax.random.randint(jax.random.fold_in(key, 32), (partitions, F_DEV), 0, 8)
    slot_draw = jax.random.randint(jax.random.fold_in(key, 33), (partitions, F_DEV), 0, SLOTS)
    receiver = jnp.arange(partitions, dtype=jnp.int32)[:, None]
    offsets = jnp.array(PEER_OFFSETS, dtype=jnp.int32)
    block_index = jnp.minimum(choose, 3)
    source = receiver + offsets[block_index]
    present = (source >= 0) & (source < partitions) & (choose < 4)
    slot_limit = counts[jnp.clip(source, 0, partitions - 1), block_index]
    slot_index = slot_draw % slot_limit
    ghost_id = C_DEV + block_index * SLOTS + slot_index
    result = jnp.where(present, ghost_id, owned_id)
    result = result.at[0, 0].set(0).at[0, 2].set(C_DEV + 4 * SLOTS - 1)
    return result.reshape(FACES).astype(jnp.int32)


def draw_face_count(key, part):
    partitions = FACES // F_DEV
    counts = jax.random.randint(jax.random.fold_in(key, 41), (partitions,), F_DEV // 2, F_DEV + 1)
    fullest = jax.random.randint(jax.random.fold_in(key, 42), (), 0, partitions)
    return counts.at[fullest].set(F_DEV).astype(jnp.int32)


def touch_ends(drawn, own_key, smallest, largest):
    index_at = [jax.random.randint(jax.random.fold_in(own_key, axis), (), 0, length) for axis, length in enumerate(drawn.shape)]
    main_axis = drawn.shape.index(max(drawn.shape))
    neighbour = index_at[:main_axis] + [(index_at[main_axis] + 1) % drawn.shape[main_axis]] + index_at[main_axis + 1:]
    return drawn.at[tuple(index_at)].set(smallest).at[tuple(neighbour)].set(largest)


def levels(own_key, shape, cuts, smallest, largest):
    factor_of = 1.0
    for dim, parts in cuts:
        heights = jax.random.uniform(jax.random.fold_in(jax.random.fold_in(own_key, 6), dim), (parts,), jnp.float32, smallest / len(cuts), largest / len(cuts))
        factor_of = factor_of * jnp.repeat(jnp.exp(heights), shape[dim] // parts).reshape((-1,) + (1,) * (len(shape) - 1 - dim))
    return factor_of


def scatter_about(rng, shape, deviation, reach, cuts=(), held_as=jnp.bfloat16):
    values = jax.random.normal(rng, shape, jnp.float32) * deviation
    if len(cuts) > 0:
        values = levels(rng, shape, cuts, -0.22, 0.18) * values
    return jnp.clip(values, min=-reach, max=reach).astype(held_as)


def setup_inputs(seed: int = 0) -> dict:
    key_list = jax.random.split(jax.random.key(seed), 11)
    state = draw_state(jax.random.fold_in(key_list[10], 71), 0)
    cell_volume = jnp.clip(jnp.exp(math.log(4.0) - 1.3862944 * jax.random.uniform(key_list[1], (CELLS,), jnp.float32) ** levels(key_list[1], (CELLS,), ((0, 8),), -0.2, 0.2)), 1.0, 4.0)
    step_size = jnp.clip(jnp.exp(math.log(0.1) - 1.609438 * jax.random.uniform(key_list[2], (CELLS,), jnp.float32) ** levels(key_list[2], (CELLS,), ((0, 8),), -0.2, 0.2)), 0.02, 0.1)
    face_normal = scatter_about(key_list[3], (3, FACES), 0.4, 1.0, ((1, 8),), jnp.float32)
    owner_arm = scatter_about(key_list[4], (3, FACES), 0.03, 0.09, ((1, 8),), jnp.float32)
    neighbor_arm = scatter_about(key_list[5], (3, FACES), 0.03, 0.09, ((1, 8),), jnp.float32)
    face_owner = draw_face_owner(jax.random.fold_in(key_list[10], 71), 0)
    face_neighbor = draw_face_neighbor(jax.random.fold_in(key_list[10], 71), 0)
    face_count = draw_face_count(jax.random.fold_in(key_list[10], 71), 0)
    send_cells = touch_ends(jax.random.randint(key_list[9], (LISTS, SLOTS), 0, C_DEV), jax.random.fold_in(key_list[9], 1), 0, C_DEV - 1).astype(jnp.int32)
    return {"state": state, "cell_volume": cell_volume, "step_size": step_size, "face_normal": face_normal, "owner_arm": owner_arm, "neighbor_arm": neighbor_arm, "face_owner": face_owner, "face_neighbor": face_neighbor, "face_count": face_count, "send_cells": send_cells}


HEAT_RATIO = 1.4
FREQUENCY = 0.5
PEER_OFFSETS = (-2, -1, 1, 2)

def spectral_table(points):
    indices = jnp.arange(points, dtype=jnp.int32)
    distance = indices[:, None] - indices[None, :]
    nonzero = jnp.where(distance == 0, 1, distance)
    signs = jnp.where(distance % 2 == 0, 1.0, -1.0)
    entries = 0.5 * signs / jnp.tan(jnp.pi * nonzero.astype(jnp.float32) / points)
    return jnp.where(distance == 0, 0.0, entries).astype(jnp.float32)

def extend_field(by_partition, partition, send_rows):
    partitions = by_partition.shape[-2]
    blocks = [jnp.take(by_partition, partition, axis=-2)]
    for position, offset in enumerate(PEER_OFFSETS):
        source = partition + offset
        present = ((source >= 0) & (source < partitions)).astype(by_partition.dtype)
        clipped = jnp.clip(source, 0, partitions - 1).astype(jnp.int32)
        send_row = send_rows[clipped, position]
        ghost_block = jnp.take(jnp.take(by_partition, clipped, axis=-2), send_row, axis=-1)
        blocks.append(ghost_block * present)
    return jnp.concatenate(blocks, axis=-1)

def cell_gradient(extended, owners, neighbors, live_mask, normals, volume):
    cell_total = volume.shape[0]
    left_state = jnp.take(extended, owners, axis=-1)
    right_state = jnp.take(extended, neighbors, axis=-1)
    half_jump = 0.5 * (right_state - left_state) * live_mask
    face_flow = half_jump[None] * normals[:, None, None, :]
    summed = jnp.zeros(face_flow.shape[:-1] + (cell_total,), face_flow.dtype)
    summed = summed.at[..., owners].add(face_flow)
    summed = summed.at[..., neighbors].add(face_flow, mode='drop')
    return summed / volume

def euler_flux(conserved, normals):
    density = conserved[0]
    momentum = conserved[1:4]
    velocity = momentum / density
    pressure = (HEAT_RATIO - 1.0) * (conserved[4] - 0.5 * lax.optimization_barrier(jnp.sum(momentum * velocity, axis=0)))
    normal_speed = lax.optimization_barrier(jnp.sum(velocity * normals[:, None, :], axis=0))
    face_area = jnp.sqrt(lax.optimization_barrier(jnp.sum(normals * normals, axis=0)))
    face_flux = jnp.concatenate([(density * normal_speed)[None], momentum * normal_speed + pressure * normals[:, None, :], ((conserved[4] + pressure) * normal_speed)[None]], axis=0)
    sound_speed = jnp.sqrt(HEAT_RATIO * pressure / density)
    return (face_flux, jnp.abs(normal_speed) + sound_speed * face_area)

def flux_residual(extended, ext_grad, owners, neighbors, live_mask, normals, owner_arm, neighbor_arm, volume):
    cell_total = volume.shape[0]
    left_state = jnp.take(extended, owners, axis=-1) + lax.optimization_barrier(jnp.sum(jnp.take(ext_grad, owners, axis=-1) * owner_arm[:, None, None, :], axis=0))
    right_state = jnp.take(extended, neighbors, axis=-1) + lax.optimization_barrier(jnp.sum(jnp.take(ext_grad, neighbors, axis=-1) * neighbor_arm[:, None, None, :], axis=0))
    flux_left, speed_left = euler_flux(left_state, normals)
    flux_right, speed_right = euler_flux(right_state, normals)
    wave_speed = jnp.maximum(speed_left, speed_right)
    face_flux = (0.5 * (flux_left + flux_right) - 0.5 * wave_speed * (right_state - left_state)) * live_mask
    summed = jnp.zeros(face_flux.shape[:-1] + (cell_total,), face_flux.dtype)
    summed = summed.at[..., owners].add(face_flux)
    summed = summed.at[..., neighbors].add(-face_flux, mode='drop')
    return summed / volume

def reference(state, cell_volume, step_size, face_normal, owner_arm, neighbor_arm, face_owner, face_neighbor, face_count, send_cells):
    owners = face_owner.reshape(-1, F_DEV)
    neighbors = face_neighbor.reshape(-1, F_DEV)
    normals = face_normal.reshape(3, -1, F_DEV)
    owner_arms = owner_arm.reshape(3, -1, F_DEV)
    neighbor_arms = neighbor_arm.reshape(3, -1, F_DEV)
    volumes = cell_volume.reshape(-1, C_DEV)
    send_rows = send_cells.reshape(-1, 4, SLOTS)
    partitions = volumes.shape[0]
    numbers = jnp.arange(partitions, dtype=jnp.int32)
    face_index = jnp.arange(F_DEV, dtype=jnp.int32)

    def section_residual(current):
        by_partition = current.reshape(NVAR, INST, partitions, C_DEV)

        def live_of(partition):
            return (face_index < face_count[partition]).astype(current.dtype)

        def partition_gradient(partition):
            extended = extend_field(by_partition, partition, send_rows)
            return cell_gradient(extended, owners[partition], neighbors[partition], live_of(partition), normals[:, partition], volumes[partition])
        gradients = lax.map(partition_gradient, numbers)
        grad_parts = jnp.moveaxis(gradients, 0, -2)

        def partition_residual(partition):
            extended = extend_field(by_partition, partition, send_rows)
            ext_grad = extend_field(grad_parts, partition, send_rows)
            return flux_residual(extended, ext_grad, owners[partition], neighbors[partition], live_of(partition), normals[:, partition], owner_arms[:, partition], neighbor_arms[:, partition], volumes[partition])
        spatial = lax.map(partition_residual, numbers)
        spatial = jnp.moveaxis(spatial, 0, -2).reshape(NVAR, INST, CELLS)
        derivative = spectral_table(INST).astype(current.dtype)
        source_term = jnp.einsum('ij,vjc->vic', derivative, current, precision=lax.Precision.HIGHEST)
        return spatial + FREQUENCY * source_term
    section_state = state - 0.5 * step_size * section_residual(state)
    residual = section_residual(section_state)
    new_state = state - step_size * residual
    return (new_state, residual)
```

```python
import functools

import jax
import jax.numpy as jnp
import numpy as np
from jax import lax
from jax.experimental import pallas as pl
from jax.experimental.pallas import tpu as pltpu
from jax.sharding import PartitionSpec as P

HEAT_RATIO = 1.4
FREQUENCY = 0.5
PEER_OFFSETS = (-2, -1, 1, 2)
MESH = pl.DeviceIdType.MESH
BF = jnp.bfloat16
F32 = jnp.float32


def spectral_matrix(points, inst_dev, nvar, rows):
    peers = points // inst_dev
    table = np.zeros((rows, peers * rows))
    for k in range(peers):
        for v in range(nvar):
            for t in range(inst_dev):
                for j in range(inst_dev):
                    d = (t - j - k * inst_dev) % points
                    if d:
                        table[v * inst_dev + t, k * rows + v * inst_dev + j] = (
                            0.5 * (-1.0) ** d / np.tan(np.pi * d / points)
                        )
    table = table.astype(np.float32)
    high = table.astype(jnp.bfloat16).astype(np.float32)
    low = table - high
    return np.concatenate([high, high, low], axis=1).astype(jnp.bfloat16)


def parts(x):
    high = x.astype(BF).astype(F32)
    return jnp.concatenate([x, x - high], axis=0).astype(BF)


def joined(y):
    half = y.shape[0] // 2
    return y[:half] + y[half:]


def mm(a, b):
    return lax.dot_general(a, b, (((1,), (0,)), ((), ())), preferred_element_type=F32)


def mm_nt(a, b):
    return lax.dot_general(a, b, (((1,), (1,)), ((), ())), preferred_element_type=F32)


def euler_flux(u, n, area):
    rho, m1, m2, m3, energy = u
    inv = 1.0 / rho
    u1, u2, u3 = m1 * inv, m2 * inv, m3 * inv
    pressure = (HEAT_RATIO - 1.0) * (energy - 0.5 * (m1 * u1 + m2 * u2 + m3 * u3))
    q = u1 * n[0] + u2 * n[1] + u3 * n[2]
    flux = (
        rho * q,
        m1 * q + pressure * n[0],
        m2 * q + pressure * n[1],
        m3 * q + pressure * n[2],
        (energy + pressure) * q,
    )
    speed = jnp.abs(q) + jnp.sqrt(HEAT_RATIO * pressure * inv) * area
    return flux, speed


def kernel(
    dims,
    state_ref, volume_ref, step_ref, normal_ref, oarm_ref, narm_ref, owner_ref, neighbor_ref,
    count_ref, send_ref, table_ref,
    new_ref, res_ref,
    own_ref, peer_ref, payv_ref, payg_ref, gv_ref, gg_ref,
    st_ref, ot_ref, nt_ref, pm_ref, dm_ref, left_ref, right_ref, acc_ref,
    sv_send, sv_recv, sg_send, sg_recv, sp_send, sp_recv,
):
    ndom, ninst, nvar, idev, cells, slots, chunks, chunk, rows = dims
    ghosts = 4 * slots
    me = lax.axis_index("dom")
    mi = lax.axis_index("inst")

    def valid(p):
        return (p >= 0) & (p < ndom)

    gv_ref[...] = jnp.zeros(gv_ref.shape, F32)
    gg_ref[...] = jnp.zeros(gg_ref.shape, F32)

    barrier = pltpu.get_barrier_semaphore()
    for off in PEER_OFFSETS:
        @pl.when(valid(me + off))
        def _(off=off):
            pl.semaphore_signal(barrier, inc=1, device_id={"dom": me + off}, device_id_type=MESH)
    for k in range(1, ninst):
        pl.semaphore_signal(
            barrier, inc=1, device_id={"inst": lax.rem(mi + k, ninst)}, device_id_type=MESH
        )

    def ghost_copy(pay, dst, send, recv, sec, k, partition):
        return pltpu.make_async_remote_copy(
            src_ref=pay.at[sec, k // 2],
            dst_ref=dst.at[sec, k],
            send_sem=send.at[sec, k],
            recv_sem=recv.at[sec, k],
            device_id={"dom": partition},
            device_id_type=MESH,
        )

    def ghosts_start(args, sec):
        for k, off in enumerate(PEER_OFFSETS):
            @pl.when(valid(me - off))
            def _(k=k, off=off):
                ghost_copy(*args, sec, k, me - off).start()

    def ghosts_wait(args, sec):
        for k, off in enumerate(PEER_OFFSETS):
            @pl.when(valid(me + off))
            def _(k=k, off=off):
                ghost_copy(*args, sec, k, me + off).wait_recv()

    def ghosts_sent(args, sec):
        for k, off in enumerate(PEER_OFFSETS):
            @pl.when(valid(me - off))
            def _(k=k, off=off):
                ghost_copy(*args, sec, k, me - off).wait_send()

    def peer_copy(sec, k):
        return pltpu.make_async_remote_copy(
            src_ref=own_ref.at[sec],
            dst_ref=peer_ref.at[sec, k - 1],
            send_sem=sp_send.at[sec, k - 1],
            recv_sem=sp_recv.at[sec, k - 1],
            device_id={"inst": lax.rem(mi + ninst - k, ninst)},
            device_id_type=MESH,
        )

    vargs = (payv_ref, gv_ref, sv_send, sv_recv)
    gargs = (payg_ref, gg_ref, sg_send, sg_recv)

    cell_id = lax.broadcasted_iota(jnp.int32, (cells, slots), 0)
    for k in range(4):
        hit = cell_id == send_ref[k:k + 1, :]
        st_ref[:, k * slots:(k + 1) * slots] = jnp.where(hit, 1.0, 0.0).astype(BF)

    pad = rows - nvar * idev
    filler = [jnp.zeros((pad, cells), F32)] if pad else []
    current = jnp.concatenate([state_ref[v] for v in range(nvar)] + filler, axis=0)
    own_ref[0] = current
    split = parts(current)

    def fill_payload(pay, sec, values):
        for j in range(2):
            pay[sec, j] = values[:, j * 2 * slots:(j + 1) * 2 * slots]

    fill_payload(payv_ref, 0, joined(mm(split, st_ref[...])))

    neighbours = sum(valid(me + off).astype(jnp.int32) for off in PEER_OFFSETS)
    pl.semaphore_wait(barrier, neighbours + (ninst - 1))

    ghosts_start(vargs, 0)
    for k in range(1, ninst):
        peer_copy(0, k).start()

    def build(c, carry):
        at = pl.ds(pl.multiple_of(c * chunk, chunk), chunk)
        ids = lax.broadcasted_iota(jnp.int32, (cells, chunk), 0)
        gids = lax.broadcasted_iota(jnp.int32, (ghosts, chunk), 0) + cells
        own = owner_ref[:, at]
        nbr = neighbor_ref[:, at]
        o = jnp.where(ids == own, 1.0, 0.0)
        n = jnp.where(ids == nbr, 1.0, 0.0)
        ot_ref[c] = o.astype(BF)
        nt_ref[c, :cells] = n.astype(BF)
        nt_ref[c, cells:] = jnp.where(gids == nbr, 1.0, 0.0).astype(BF)
        pm_ref[c] = (o + n).astype(BF)
        dm_ref[c] = (o - n).astype(BF)
        return carry

    lax.fori_loop(0, chunks, build, 0)

    inv_volume = 1.0 / volume_ref[...]
    lane = lax.broadcasted_iota(jnp.int32, (1, chunk), 1)
    half = chunk // 2
    low_rows = lax.broadcasted_iota(jnp.int32, (2 * idev, half), 0) < idev

    def packed(x, v):
        tile = x[(v // 2) * 2 * idev:(v // 2 + 1) * 2 * idev]
        a, b = tile[:, :half], tile[:, half:]
        if v % 2 == 0:
            return jnp.where(low_rows, a, pltpu.roll(b, idev, 0))
        return jnp.where(low_rows, pltpu.roll(a, idev, 0), b)

    def unpacked(even, odd):
        if odd is None:
            a = jnp.where(low_rows, even, 0.0)
            b = jnp.where(low_rows, pltpu.roll(even, idev, 0), 0.0)
        else:
            a = jnp.where(low_rows, even, pltpu.roll(odd, idev, 0))
            b = jnp.where(low_rows, pltpu.roll(even, idev, 0), odd)
        return jnp.concatenate([a, b], axis=1)

    def both_halves(x):
        return jnp.where(low_rows, x[:, :half], x[:, half:])

    def ghost_values(ref, sec):
        wide = ref.shape[-2]
        first = lax.broadcasted_iota(jnp.int32, (wide, 2 * slots), 1) < slots
        return jnp.concatenate(
            [jnp.where(first, ref[sec, 2 * j], ref[sec, 2 * j + 1]) for j in range(2)], axis=1
        )

    def section(sec, split):
        def gather_local(c, carry):
            left_ref[c] = joined(mm(split, ot_ref[c]))
            right_ref[c] = joined(mm(split, nt_ref[c, :cells]))
            return carry

        lax.fori_loop(0, chunks, gather_local, 0)
        ghosts_wait(vargs, sec)
        gsplit = parts(ghost_values(gv_ref, sec))
        acc_ref[...] = jnp.zeros(acc_ref.shape, F32)

        def gradient_step(c, carry):
            at = pl.ds(pl.multiple_of(c * chunk, chunk), chunk)
            right = right_ref[c] + joined(mm(gsplit, nt_ref[c, cells:]))
            right_ref[c] = right
            live = (lane + c * chunk) < count_ref[0]
            jump = jnp.where(live, 0.5 * (right - left_ref[c]), 0.0)
            flow = jnp.concatenate([jump * normal_ref[d:d + 1, at] for d in range(3)], axis=0)
            acc_ref[...] += joined(mm_nt(parts(flow), pm_ref[c]))
            return carry

        lax.fori_loop(0, chunks, gradient_step, 0)
        gradient = acc_ref[...] * inv_volume
        dsplit = parts(gradient)
        fill_payload(payg_ref, sec, joined(mm(dsplit, st_ref[...])))
        ghosts_start(gargs, sec)

        def reconstruct(c, carry):
            at = pl.ds(pl.multiple_of(c * chunk, chunk), chunk)
            left = joined(mm(dsplit, ot_ref[c]))
            right = joined(mm(dsplit, nt_ref[c, :cells]))
            tl, tr = left_ref[c], right_ref[c]
            for d in range(3):
                tl = tl + left[d * rows:(d + 1) * rows] * oarm_ref[d:d + 1, at]
                tr = tr + right[d * rows:(d + 1) * rows] * narm_ref[d:d + 1, at]
            left_ref[c] = tl
            right_ref[c] = tr
            return carry

        lax.fori_loop(0, chunks, reconstruct, 0)

        for k in range(1, ninst):
            peer_copy(sec, k).wait_recv()
        every = jnp.concatenate(
            [own_ref[sec]] + [peer_ref[sec, k - 1] for k in range(1, ninst)], axis=0
        )
        high = every.astype(BF).astype(F32)
        stacked = jnp.concatenate([every, every - high, every], axis=0).astype(BF)
        spectral = mm(table_ref[...], stacked)

        ghosts_wait(gargs, sec)
        hsplit = parts(ghost_values(gg_ref, sec))
        acc_ref[:rows] = jnp.zeros((rows, cells), F32)

        def flux_step(c, carry):
            at = pl.ds(pl.multiple_of(c * chunk, chunk), chunk)
            extra = joined(mm(hsplit, nt_ref[c, cells:]))
            tl, tr = left_ref[c], right_ref[c]
            for d in range(3):
                tr = tr + extra[d * rows:(d + 1) * rows] * narm_ref[d:d + 1, at]
            normals = [both_halves(normal_ref[d:d + 1, at]) for d in range(3)]
            area = jnp.sqrt(
                normals[0] * normals[0] + normals[1] * normals[1] + normals[2] * normals[2]
            )
            ul = [packed(tl, v) for v in range(nvar)]
            ur = [packed(tr, v) for v in range(nvar)]
            fl, sl = euler_flux(ul, normals, area)
            fr, sr = euler_flux(ur, normals, area)
            wave = jnp.maximum(sl, sr)
            flux = [
                0.5 * ((fl[v] + fr[v]) - wave * (ur[v] - ul[v])) for v in range(nvar)
            ] + [None]
            face = jnp.concatenate(
                [unpacked(flux[2 * j], flux[2 * j + 1]) for j in range((nvar + 1) // 2)], axis=0
            )
            live = (lane + c * chunk) < count_ref[0]
            face = jnp.where(live, face, 0.0)
            acc_ref[:rows] += joined(mm_nt(parts(face), dm_ref[c]))
            return carry

        lax.fori_loop(0, chunks, flux_step, 0)
        return acc_ref[:rows] * inv_volume + FREQUENCY * spectral

    step = step_ref[...]
    current = current - 0.5 * step * section(0, split)
    own_ref[1] = current
    for k in range(1, ninst):
        peer_copy(1, k).start()
    split = parts(current)
    fill_payload(payv_ref, 1, joined(mm(split, st_ref[...])))
    ghosts_start(vargs, 1)
    residual = section(1, split)
    new = own_ref[0] - step * residual
    for v in range(nvar):
        new_ref[v] = new[v * idev:(v + 1) * idev]
        res_ref[v] = residual[v * idev:(v + 1) * idev]

    for sec in range(2):
        ghosts_sent(vargs, sec)
        ghosts_sent(gargs, sec)
        for k in range(1, ninst):
            peer_copy(sec, k).wait_send()


def solution(mesh):
    ndom, ninst = mesh.shape["dom"], mesh.shape["inst"]

    def local(
        state, cell_volume, step_size, face_normal, owner_arm, neighbor_arm,
        face_owner, face_neighbor, face_count, send_cells,
    ):
        nvar, idev, cells = state.shape
        faces = face_owner.shape[0]
        slots = send_cells.shape[1]
        chunk = min(512, faces)
        chunks = faces // chunk
        rows = -(-nvar * idev // 8) * 8
        ghosts = 4 * slots
        dims = (ndom, ninst, nvar, idev, cells, slots, chunks, chunk, rows)
        table = jnp.asarray(spectral_matrix(idev * ninst, idev, nvar, rows))
        vmem = pl.BlockSpec(memory_space=pltpu.VMEM)
        smem = pl.BlockSpec(memory_space=pltpu.SMEM)
        shape = jax.ShapeDtypeStruct(state.shape, F32)
        dma = pltpu.SemaphoreType.DMA
        return pl.pallas_call(
            functools.partial(kernel, dims),
            out_shape=(shape, shape),
            in_specs=[vmem] * 8 + [smem] + [vmem] * 2,
            out_specs=(vmem, vmem),
            scratch_shapes=[
                pltpu.VMEM((2, rows, cells), F32),
                pltpu.VMEM((2, ninst - 1, rows, cells), F32),
                pltpu.VMEM((2, 2, rows, 2 * slots), F32),
                pltpu.VMEM((2, 2, 3 * rows, 2 * slots), F32),
                pltpu.VMEM((2, 4, rows, 2 * slots), F32),
                pltpu.VMEM((2, 4, 3 * rows, 2 * slots), F32),
                pltpu.VMEM((cells, ghosts), BF),
                pltpu.VMEM((chunks, cells, chunk), BF),
                pltpu.VMEM((chunks, cells + ghosts, chunk), BF),
                pltpu.VMEM((chunks, cells, chunk), BF),
                pltpu.VMEM((chunks, cells, chunk), BF),
                pltpu.VMEM((chunks, rows, chunk), F32),
                pltpu.VMEM((chunks, rows, chunk), F32),
                pltpu.VMEM((3 * rows, cells), F32),
                dma((2, 4)), dma((2, 4)), dma((2, 4)), dma((2, 4)),
                dma((2, ninst - 1)), dma((2, ninst - 1)),
            ],
            compiler_params=pltpu.CompilerParams(
                collective_id=0, has_side_effects=True, vmem_limit_bytes=40 * 1024 * 1024
            ),
        )(
            state, cell_volume[None], step_size[None], face_normal, owner_arm, neighbor_arm,
            face_owner[None], face_neighbor[None], face_count, send_cells, table,
        )

    placed = (
        P(None, "inst", "dom"),
        P("dom"),
        P("dom"),
        P(None, "dom"),
        P(None, "dom"),
        P(None, "dom"),
        P("dom"),
        P("dom"),
        P("dom"),
        P("dom", None),
    )
    return jax.shard_map(
        local,
        mesh=mesh,
        in_specs=placed,
        out_specs=(P(None, "inst", "dom"), P(None, "inst", "dom")),
        check_vma=False,
    )
```

```python
import functools

import jax
import jax.numpy as jnp
import numpy as np
from jax import lax
from jax.experimental import pallas as pl
from jax.experimental.pallas import tpu as pltpu
from jax.sharding import PartitionSpec as P

HEAT_RATIO = 1.4
FREQUENCY = 0.5
PEER_OFFSETS = (-2, -1, 1, 2)
MESH = pl.DeviceIdType.MESH
BF = jnp.bfloat16
F32 = jnp.float32


def spectral_matrix(points, inst_dev, nvar, rows):
    peers = points // inst_dev
    table = np.zeros((rows, peers * rows))
    for k in range(peers):
        for v in range(nvar):
            for t in range(inst_dev):
                for j in range(inst_dev):
                    d = (t - j - k * inst_dev) % points
                    if d:
                        table[v * inst_dev + t, k * rows + v * inst_dev + j] = (
                            0.5 * (-1.0) ** d / np.tan(np.pi * d / points)
                        )
    table = table.astype(np.float32)
    high = table.astype(jnp.bfloat16).astype(np.float32)
    low = table - high
    return np.concatenate([high, high, low], axis=1).astype(jnp.bfloat16)


def parts(x):
    high = x.astype(BF).astype(F32)
    return jnp.concatenate([x, x - high], axis=0).astype(BF)


def joined(y):
    half = y.shape[0] // 2
    return y[:half] + y[half:]


def mm(a, b):
    return lax.dot_general(a, b, (((1,), (0,)), ((), ())), preferred_element_type=F32)


def mm_nt(a, b):
    return lax.dot_general(a, b, (((1,), (1,)), ((), ())), preferred_element_type=F32)


def euler_flux(u, n, area):
    rho, m1, m2, m3, energy = u
    inv = 1.0 / rho
    u1, u2, u3 = m1 * inv, m2 * inv, m3 * inv
    pressure = (HEAT_RATIO - 1.0) * (energy - 0.5 * (m1 * u1 + m2 * u2 + m3 * u3))
    q = u1 * n[0] + u2 * n[1] + u3 * n[2]
    flux = (
        rho * q,
        m1 * q + pressure * n[0],
        m2 * q + pressure * n[1],
        m3 * q + pressure * n[2],
        (energy + pressure) * q,
    )
    speed = jnp.abs(q) + jnp.sqrt(HEAT_RATIO * pressure * inv) * area
    return flux, speed


def kernel(
    dims,
    state_hbm, volume_hbm, step_hbm, normal_hbm, oarm_hbm, narm_hbm, owner_hbm, neighbor_hbm,
    count_hbm, send_hbm, table_hbm,
    new_ref, res_ref,
    state_ref, volume_ref, step_ref, normal_ref, oarm_ref, narm_ref, owner_ref, neighbor_ref,
    count_ref, send_ref, table_ref, in_sem,
    own_ref, peer_ref, payv_ref, payg_ref, gv_ref, gg_ref,
    st_ref, ot_ref, nt_ref, pm_ref, dm_ref, left_ref, right_ref, acc_ref,
    sv_send, sv_recv, sg_send, sg_recv, sp_send, sp_recv,
):
    ndom, ninst, nvar, idev, cells, slots, chunks, chunk, rows = dims
    ghosts = 4 * slots
    me = lax.axis_index("dom")
    mi = lax.axis_index("inst")

    def valid(p):
        return (p >= 0) & (p < ndom)

    fetches = [
        pltpu.make_async_copy(source, target, in_sem.at[i])
        for i, (source, target) in enumerate((
            (state_hbm, state_ref), (send_hbm, send_ref),
            (owner_hbm, owner_ref), (neighbor_hbm, neighbor_ref),
            (volume_hbm, volume_ref), (count_hbm, count_ref), (normal_hbm, normal_ref),
            (oarm_hbm, oarm_ref), (narm_hbm, narm_ref),
            (step_hbm, step_ref), (table_hbm, table_ref),
        ))
    ]
    for fetch in fetches:
        fetch.start()
    gv_ref[...] = jnp.zeros(gv_ref.shape, F32)
    gg_ref[...] = jnp.zeros(gg_ref.shape, F32)

    barrier = pltpu.get_barrier_semaphore()
    for off in PEER_OFFSETS:
        @pl.when(valid(me + off))
        def _(off=off):
            pl.semaphore_signal(barrier, inc=1, device_id={"dom": me + off}, device_id_type=MESH)
    for k in range(1, ninst):
        pl.semaphore_signal(
            barrier, inc=1, device_id={"inst": lax.rem(mi + k, ninst)}, device_id_type=MESH
        )

    def ghost_copy(pay, dst, send, recv, sec, k, partition):
        return pltpu.make_async_remote_copy(
            src_ref=pay.at[sec, k // 2],
            dst_ref=dst.at[sec, k],
            send_sem=send.at[sec, k],
            recv_sem=recv.at[sec, k],
            device_id={"dom": partition},
            device_id_type=MESH,
        )

    def ghosts_start(args, sec):
        for k, off in enumerate(PEER_OFFSETS):
            @pl.when(valid(me - off))
            def _(k=k, off=off):
                ghost_copy(*args, sec, k, me - off).start()

    def ghosts_wait(args, sec):
        for k, off in enumerate(PEER_OFFSETS):
            @pl.when(valid(me + off))
            def _(k=k, off=off):
                ghost_copy(*args, sec, k, me + off).wait_recv()

    def ghosts_sent(args, sec):
        for k, off in enumerate(PEER_OFFSETS):
            @pl.when(valid(me - off))
            def _(k=k, off=off):
                ghost_copy(*args, sec, k, me - off).wait_send()

    def peer_copy(sec, k):
        return pltpu.make_async_remote_copy(
            src_ref=own_ref.at[sec],
            dst_ref=peer_ref.at[sec, k - 1],
            send_sem=sp_send.at[sec, k - 1],
            recv_sem=sp_recv.at[sec, k - 1],
            device_id={"inst": lax.rem(mi + ninst - k, ninst)},
            device_id_type=MESH,
        )

    vargs = (payv_ref, gv_ref, sv_send, sv_recv)
    gargs = (payg_ref, gg_ref, sg_send, sg_recv)

    for fetch in fetches[:2]:
        fetch.wait()
    cell_id = lax.broadcasted_iota(jnp.int32, (cells, slots), 0)
    for k in range(4):
        hit = cell_id == send_ref[k:k + 1, :]
        st_ref[:, k * slots:(k + 1) * slots] = jnp.where(hit, 1.0, 0.0).astype(BF)

    pad = rows - nvar * idev
    filler = [jnp.zeros((pad, cells), F32)] if pad else []
    current = jnp.concatenate([state_ref[v] for v in range(nvar)] + filler, axis=0)
    own_ref[0] = current
    split = parts(current)

    def fill_payload(pay, sec, values):
        for j in range(2):
            pay[sec, j] = values[:, j * 2 * slots:(j + 1) * 2 * slots]

    fill_payload(payv_ref, 0, joined(mm(split, st_ref[...])))

    neighbours = sum(valid(me + off).astype(jnp.int32) for off in PEER_OFFSETS)
    pl.semaphore_wait(barrier, neighbours + (ninst - 1))

    ghosts_start(vargs, 0)
    for k in range(1, ninst):
        peer_copy(0, k).start()

    for fetch in fetches[2:]:
        fetch.wait()
    def build(c, carry):
        at = pl.ds(pl.multiple_of(c * chunk, chunk), chunk)
        ids = lax.broadcasted_iota(jnp.int32, (cells, chunk), 0)
        gids = lax.broadcasted_iota(jnp.int32, (ghosts, chunk), 0) + cells
        own = owner_ref[:, at]
        nbr = neighbor_ref[:, at]
        o = jnp.where(ids == own, 1.0, 0.0).astype(BF)
        n = jnp.where(ids == nbr, 1.0, 0.0).astype(BF)
        ot_ref[c] = o
        nt_ref[c, :cells] = n
        nt_ref[c, cells:] = jnp.where(gids == nbr, 1.0, 0.0).astype(BF)
        pm_ref[c] = o + n
        dm_ref[c] = o - n
        return carry

    lax.fori_loop(0, chunks, build, 0)

    inv_volume = 1.0 / volume_ref[...]
    lane = lax.broadcasted_iota(jnp.int32, (1, chunk), 1)
    half = chunk // 2
    low_rows = lax.broadcasted_iota(jnp.int32, (2 * idev, half), 0) < idev

    def packed(x, v):
        tile = x[(v // 2) * 2 * idev:(v // 2 + 1) * 2 * idev]
        a, b = tile[:, :half], tile[:, half:]
        if v % 2 == 0:
            return jnp.where(low_rows, a, pltpu.roll(b, idev, 0))
        return jnp.where(low_rows, pltpu.roll(a, idev, 0), b)

    def unpacked(even, odd):
        if odd is None:
            a = jnp.where(low_rows, even, 0.0)
            b = jnp.where(low_rows, pltpu.roll(even, idev, 0), 0.0)
        else:
            a = jnp.where(low_rows, even, pltpu.roll(odd, idev, 0))
            b = jnp.where(low_rows, pltpu.roll(even, idev, 0), odd)
        return jnp.concatenate([a, b], axis=1)

    def both_halves(x):
        return jnp.where(low_rows, x[:, :half], x[:, half:])

    def ghost_values(ref, sec):
        wide = ref.shape[-2]
        first = lax.broadcasted_iota(jnp.int32, (wide, 2 * slots), 1) < slots
        return jnp.concatenate(
            [jnp.where(first, ref[sec, 2 * j], ref[sec, 2 * j + 1]) for j in range(2)], axis=1
        )

    def section(sec, split):
        def gather_local(c, carry):
            left_ref[c] = joined(mm(split, ot_ref[c]))
            right_ref[c] = joined(mm(split, nt_ref[c, :cells]))
            return carry

        lax.fori_loop(0, chunks, gather_local, 0)
        ghosts_wait(vargs, sec)
        gsplit = parts(ghost_values(gv_ref, sec))
        acc_ref[...] = jnp.zeros(acc_ref.shape, F32)

        def gradient_step(c, carry):
            at = pl.ds(pl.multiple_of(c * chunk, chunk), chunk)
            right = right_ref[c] + joined(mm(gsplit, nt_ref[c, cells:]))
            right_ref[c] = right
            live = (lane + c * chunk) < count_ref[...]
            jump = jnp.where(live, 0.5 * (right - left_ref[c]), 0.0)
            flow = jnp.concatenate([jump * normal_ref[d:d + 1, at] for d in range(3)], axis=0)
            acc_ref[...] += joined(mm_nt(parts(flow), pm_ref[c]))
            return carry

        lax.fori_loop(0, chunks, gradient_step, 0)
        gradient = acc_ref[...] * inv_volume
        dsplit = parts(gradient)
        fill_payload(payg_ref, sec, joined(mm(dsplit, st_ref[...])))
        ghosts_start(gargs, sec)

        def reconstruct(c, carry):
            at = pl.ds(pl.multiple_of(c * chunk, chunk), chunk)
            left = joined(mm(dsplit, ot_ref[c]))
            right = joined(mm(dsplit, nt_ref[c, :cells]))
            tl, tr = left_ref[c], right_ref[c]
            for d in range(3):
                tl = tl + left[d * rows:(d + 1) * rows] * oarm_ref[d:d + 1, at]
                tr = tr + right[d * rows:(d + 1) * rows] * narm_ref[d:d + 1, at]
            left_ref[c] = tl
            right_ref[c] = tr
            return carry

        lax.fori_loop(0, chunks, reconstruct, 0)

        for k in range(1, ninst):
            peer_copy(sec, k).wait_recv()
        every = jnp.concatenate(
            [own_ref[sec]] + [peer_ref[sec, k - 1] for k in range(1, ninst)], axis=0
        )
        high = every.astype(BF).astype(F32)
        stacked = jnp.concatenate([every, every - high, every], axis=0).astype(BF)
        spectral = mm(table_ref[...], stacked)

        ghosts_wait(gargs, sec)
        hsplit = parts(ghost_values(gg_ref, sec))
        acc_ref[:rows] = jnp.zeros((rows, cells), F32)

        def flux_step(c, carry):
            at = pl.ds(pl.multiple_of(c * chunk, chunk), chunk)
            extra = joined(mm(hsplit, nt_ref[c, cells:]))
            tl, tr = left_ref[c], right_ref[c]
            for d in range(3):
                tr = tr + extra[d * rows:(d + 1) * rows] * narm_ref[d:d + 1, at]
            normals = [both_halves(normal_ref[d:d + 1, at]) for d in range(3)]
            area = jnp.sqrt(
                normals[0] * normals[0] + normals[1] * normals[1] + normals[2] * normals[2]
            )
            ul = [packed(tl, v) for v in range(nvar)]
            ur = [packed(tr, v) for v in range(nvar)]
            fl, sl = euler_flux(ul, normals, area)
            fr, sr = euler_flux(ur, normals, area)
            wave = jnp.maximum(sl, sr)
            flux = [
                0.5 * ((fl[v] + fr[v]) - wave * (ur[v] - ul[v])) for v in range(nvar)
            ] + [None]
            face = jnp.concatenate(
                [unpacked(flux[2 * j], flux[2 * j + 1]) for j in range((nvar + 1) // 2)], axis=0
            )
            live = (lane + c * chunk) < count_ref[...]
            face = jnp.where(live, face, 0.0)
            acc_ref[:rows] += joined(mm_nt(parts(face), dm_ref[c]))
            return carry

        lax.fori_loop(0, chunks, flux_step, 0)
        return acc_ref[:rows] * inv_volume + FREQUENCY * spectral

    step = step_ref[...]
    current = current - 0.5 * step * section(0, split)
    own_ref[1] = current
    for k in range(1, ninst):
        peer_copy(1, k).start()
    split = parts(current)
    fill_payload(payv_ref, 1, joined(mm(split, st_ref[...])))
    ghosts_start(vargs, 1)
    residual = section(1, split)
    new = own_ref[0] - step * residual
    for v in range(nvar):
        new_ref[v] = new[v * idev:(v + 1) * idev]
        res_ref[v] = residual[v * idev:(v + 1) * idev]

    for sec in range(2):
        ghosts_sent(vargs, sec)
        ghosts_sent(gargs, sec)
        for k in range(1, ninst):
            peer_copy(sec, k).wait_send()


def solution(mesh):
    ndom, ninst = mesh.shape["dom"], mesh.shape["inst"]

    def local(
        state, cell_volume, step_size, face_normal, owner_arm, neighbor_arm,
        face_owner, face_neighbor, face_count, send_cells,
    ):
        nvar, idev, cells = state.shape
        faces = face_owner.shape[0]
        slots = send_cells.shape[1]
        chunk = min(1024, faces)
        chunks = faces // chunk
        rows = -(-nvar * idev // 8) * 8
        ghosts = 4 * slots
        dims = (ndom, ninst, nvar, idev, cells, slots, chunks, chunk, rows)
        table = jnp.asarray(spectral_matrix(idev * ninst, idev, nvar, rows))
        vmem = pl.BlockSpec(memory_space=pltpu.VMEM)
        hbm = pl.BlockSpec(memory_space=pltpu.HBM)
        shape = jax.ShapeDtypeStruct(state.shape, F32)
        dma = pltpu.SemaphoreType.DMA
        return pl.pallas_call(
            functools.partial(kernel, dims),
            out_shape=(shape, shape),
            in_specs=[hbm] * 11,
            out_specs=(vmem, vmem),
            scratch_shapes=[
                pltpu.VMEM(state.shape, F32),
                pltpu.VMEM((1, cells), F32),
                pltpu.VMEM((1, cells), F32),
                pltpu.VMEM((3, faces), F32),
                pltpu.VMEM((3, faces), F32),
                pltpu.VMEM((3, faces), F32),
                pltpu.VMEM((1, faces), jnp.int32),
                pltpu.VMEM((1, faces), jnp.int32),
                pltpu.VMEM((1, 1), jnp.int32),
                pltpu.VMEM((4, slots), jnp.int32),
                pltpu.VMEM(table.shape, BF),
                dma((11,)),
                pltpu.VMEM((2, rows, cells), F32),
                pltpu.VMEM((2, ninst - 1, rows, cells), F32),
                pltpu.VMEM((2, 2, rows, 2 * slots), F32),
                pltpu.VMEM((2, 2, 3 * rows, 2 * slots), F32),
                pltpu.VMEM((2, 4, rows, 2 * slots), F32),
                pltpu.VMEM((2, 4, 3 * rows, 2 * slots), F32),
                pltpu.VMEM((cells, ghosts), BF),
                pltpu.VMEM((chunks, cells, chunk), BF),
                pltpu.VMEM((chunks, cells + ghosts, chunk), BF),
                pltpu.VMEM((chunks, cells, chunk), BF),
                pltpu.VMEM((chunks, cells, chunk), BF),
                pltpu.VMEM((chunks, rows, chunk), F32),
                pltpu.VMEM((chunks, rows, chunk), F32),
                pltpu.VMEM((3 * rows, cells), F32),
                dma((2, 4)), dma((2, 4)), dma((2, 4)), dma((2, 4)),
                dma((2, ninst - 1)), dma((2, ninst - 1)),
            ],
            compiler_params=pltpu.CompilerParams(
                collective_id=0, has_side_effects=True, vmem_limit_bytes=64 * 1024 * 1024
            ),
        )(
            state, cell_volume[None], step_size[None], face_normal, owner_arm, neighbor_arm,
            face_owner[None], face_neighbor[None], face_count[None], send_cells, table,
        )

    placed = (
        P(None, "inst", "dom"),
        P("dom"),
        P("dom"),
        P(None, "dom"),
        P(None, "dom"),
        P(None, "dom"),
        P("dom"),
        P("dom"),
        P("dom"),
        P("dom", None),
    )
    return jax.shard_map(
        local,
        mesh=mesh,
        in_specs=placed,
        out_specs=(P(None, "inst", "dom"), P(None, "inst", "dom")),
        check_vma=False,
    )
```

```python
import functools

import jax
import jax.numpy as jnp
import numpy as np
from jax import lax
from jax.experimental import pallas as pl
from jax.experimental.pallas import tpu as pltpu
from jax.sharding import PartitionSpec as P

HEAT_RATIO = 1.4
FREQUENCY = 0.5
PEER_OFFSETS = (-2, -1, 1, 2)
MESH = pl.DeviceIdType.MESH
BF = jnp.bfloat16
F32 = jnp.float32


def spectral_matrix(points, inst_dev, nvar, rows):
    peers = points // inst_dev
    table = np.zeros((rows, peers * rows))
    for k in range(peers):
        for v in range(nvar):
            for t in range(inst_dev):
                for j in range(inst_dev):
                    d = (t - j - k * inst_dev) % points
                    if d:
                        table[v * inst_dev + t, k * rows + v * inst_dev + j] = (
                            0.5 * (-1.0) ** d / np.tan(np.pi * d / points)
                        )
    table = table.astype(np.float32)
    high = table.astype(jnp.bfloat16).astype(np.float32)
    low = table - high
    return np.concatenate([high, high, low], axis=1).astype(jnp.bfloat16)


def parts(x):
    high = x.astype(BF).astype(F32)
    return jnp.concatenate([x, x - high], axis=0).astype(BF)


def joined(y):
    half = y.shape[0] // 2
    return y[:half] + y[half:]


def mm(a, b):
    return lax.dot_general(a, b, (((1,), (0,)), ((), ())), preferred_element_type=F32)


def mm_nt(a, b):
    return lax.dot_general(a, b, (((1,), (1,)), ((), ())), preferred_element_type=F32)


def euler_flux(u, n, area):
    rho, m1, m2, m3, energy = u
    inv = 1.0 / rho
    u1, u2, u3 = m1 * inv, m2 * inv, m3 * inv
    pressure = (HEAT_RATIO - 1.0) * (energy - 0.5 * (m1 * u1 + m2 * u2 + m3 * u3))
    q = u1 * n[0] + u2 * n[1] + u3 * n[2]
    flux = (
        rho * q,
        m1 * q + pressure * n[0],
        m2 * q + pressure * n[1],
        m3 * q + pressure * n[2],
        (energy + pressure) * q,
    )
    speed = jnp.abs(q) + jnp.sqrt(HEAT_RATIO * pressure * inv) * area
    return flux, speed


def kernel(
    dims,
    state_hbm, volume_hbm, step_hbm, normal_hbm, oarm_hbm, narm_hbm, owner_hbm, neighbor_hbm,
    count_hbm, send_hbm, table_hbm,
    new_ref, res_ref,
    state_ref, volume_ref, step_ref, normal_ref, oarm_ref, narm_ref, owner_ref, neighbor_ref,
    count_ref, send_ref, table_ref, in_sem,
    own_ref, peer_ref, payv_ref, payg_ref, gv_ref, gg_ref,
    st_ref, ot_ref, nt_ref, pm_ref, dm_ref, left_ref, right_ref, acc_ref,
    sv_send, sv_recv, sg_send, sg_recv, sp_send, sp_recv,
):
    ndom, ninst, nvar, idev, cells, slots, chunks, chunk, rows = dims
    ghosts = 4 * slots
    me = lax.axis_index("dom")
    mi = lax.axis_index("inst")

    def valid(p):
        return (p >= 0) & (p < ndom)

    fetches = [
        pltpu.make_async_copy(source, target, in_sem.at[i])
        for i, (source, target) in enumerate((
            (state_hbm, state_ref), (send_hbm, send_ref),
            (owner_hbm, owner_ref), (neighbor_hbm, neighbor_ref),
            (volume_hbm, volume_ref), (count_hbm, count_ref), (normal_hbm, normal_ref),
            (oarm_hbm, oarm_ref), (narm_hbm, narm_ref),
            (step_hbm, step_ref), (table_hbm, table_ref),
        ))
    ]
    for fetch in fetches:
        fetch.start()
    gv_ref[...] = jnp.zeros(gv_ref.shape, F32)
    gg_ref[...] = jnp.zeros(gg_ref.shape, F32)

    barrier = pltpu.get_barrier_semaphore()
    for off in PEER_OFFSETS:
        @pl.when(valid(me + off))
        def _(off=off):
            pl.semaphore_signal(barrier, inc=1, device_id={"dom": me + off}, device_id_type=MESH)
    for k in range(1, ninst):
        pl.semaphore_signal(
            barrier, inc=1, device_id={"inst": lax.rem(mi + k, ninst)}, device_id_type=MESH
        )

    def ghost_copy(pay, dst, send, recv, sec, k, partition):
        return pltpu.make_async_remote_copy(
            src_ref=pay.at[sec, k // 2],
            dst_ref=dst.at[sec, k],
            send_sem=send.at[sec, k],
            recv_sem=recv.at[sec, k],
            device_id={"dom": partition},
            device_id_type=MESH,
        )

    def ghosts_start(args, sec):
        for k, off in enumerate(PEER_OFFSETS):
            @pl.when(valid(me - off))
            def _(k=k, off=off):
                ghost_copy(*args, sec, k, me - off).start()

    def ghosts_wait(args, sec):
        for k, off in enumerate(PEER_OFFSETS):
            @pl.when(valid(me + off))
            def _(k=k, off=off):
                ghost_copy(*args, sec, k, me + off).wait_recv()

    def ghosts_sent(args, sec):
        for k, off in enumerate(PEER_OFFSETS):
            @pl.when(valid(me - off))
            def _(k=k, off=off):
                ghost_copy(*args, sec, k, me - off).wait_send()

    def peer_copy(sec, k):
        return pltpu.make_async_remote_copy(
            src_ref=own_ref.at[sec],
            dst_ref=peer_ref.at[sec, k - 1],
            send_sem=sp_send.at[sec, k - 1],
            recv_sem=sp_recv.at[sec, k - 1],
            device_id={"inst": lax.rem(mi + ninst - k, ninst)},
            device_id_type=MESH,
        )

    vargs = (payv_ref, gv_ref, sv_send, sv_recv)
    gargs = (payg_ref, gg_ref, sg_send, sg_recv)

    for fetch in fetches[:2]:
        fetch.wait()
    cell_id = lax.broadcasted_iota(jnp.int32, (cells, slots), 0)
    for k in range(4):
        hit = cell_id == send_ref[k:k + 1, :]
        st_ref[:, k * slots:(k + 1) * slots] = jnp.where(hit, 1.0, 0.0).astype(BF)

    pad = rows - nvar * idev
    filler = [jnp.zeros((pad, cells), F32)] if pad else []
    current = jnp.concatenate([state_ref[v] for v in range(nvar)] + filler, axis=0)
    own_ref[0] = current
    split = parts(current)

    def fill_payload(pay, sec, values):
        for j in range(2):
            pay[sec, j] = values[:, j * 2 * slots:(j + 1) * 2 * slots]

    fill_payload(payv_ref, 0, joined(mm(split, st_ref[...])))

    neighbours = sum(valid(me + off).astype(jnp.int32) for off in PEER_OFFSETS)
    pl.semaphore_wait(barrier, neighbours + (ninst - 1))

    ghosts_start(vargs, 0)
    for k in range(1, ninst):
        peer_copy(0, k).start()

    for fetch in fetches[2:]:
        fetch.wait()
    def build(c, carry):
        at = pl.ds(pl.multiple_of(c * chunk, chunk), chunk)
        ids = lax.broadcasted_iota(jnp.int32, (cells, chunk), 0)
        gids = lax.broadcasted_iota(jnp.int32, (ghosts, chunk), 0) + cells
        own = owner_ref[:, at]
        nbr = neighbor_ref[:, at]
        o = jnp.where(ids == own, 1.0, 0.0).astype(BF)
        n = jnp.where(ids == nbr, 1.0, 0.0).astype(BF)
        ot_ref[c] = o
        nt_ref[c, :cells] = n
        nt_ref[c, cells:] = jnp.where(gids == nbr, 1.0, 0.0).astype(BF)
        pm_ref[c] = o + n
        dm_ref[c] = o - n
        return carry

    lax.fori_loop(0, chunks, build, 0)

    inv_volume = 1.0 / volume_ref[...]
    lane = lax.broadcasted_iota(jnp.int32, (1, chunk), 1)
    half = chunk // 2
    low_rows = lax.broadcasted_iota(jnp.int32, (2 * idev, half), 0) < idev

    def packed(x, v):
        tile = x[(v // 2) * 2 * idev:(v // 2 + 1) * 2 * idev]
        a, b = tile[:, :half], tile[:, half:]
        if v % 2 == 0:
            return jnp.where(low_rows, a, pltpu.roll(b, idev, 0))
        return jnp.where(low_rows, pltpu.roll(a, idev, 0), b)

    def unpacked(even, odd):
        if odd is None:
            a = jnp.where(low_rows, even, 0.0)
            b = jnp.where(low_rows, pltpu.roll(even, idev, 0), 0.0)
        else:
            a = jnp.where(low_rows, even, pltpu.roll(odd, idev, 0))
            b = jnp.where(low_rows, pltpu.roll(even, idev, 0), odd)
        return jnp.concatenate([a, b], axis=1)

    def both_halves(x):
        return jnp.where(low_rows, x[:, :half], x[:, half:])

    def ghost_values(ref, sec):
        wide = ref.shape[-2]
        first = lax.broadcasted_iota(jnp.int32, (wide, 2 * slots), 1) < slots
        return jnp.concatenate(
            [jnp.where(first, ref[sec, 2 * j], ref[sec, 2 * j + 1]) for j in range(2)], axis=1
        )

    def section(sec, split):
        def gather_local(c, carry):
            left_ref[c] = joined(mm(split, ot_ref[c]))
            right_ref[c] = joined(mm(split, nt_ref[c, :cells]))
            return carry

        lax.fori_loop(0, chunks, gather_local, 0)
        ghosts_wait(vargs, sec)
        gsplit = parts(ghost_values(gv_ref, sec))
        acc_ref[...] = jnp.zeros(acc_ref.shape, F32)

        def gradient_step(c, carry):
            at = pl.ds(pl.multiple_of(c * chunk, chunk), chunk)
            right = right_ref[c] + joined(mm(gsplit, nt_ref[c, cells:]))
            right_ref[c] = right
            live = (lane + c * chunk) < count_ref[...]
            jump = jnp.where(live, 0.5 * (right - left_ref[c]), 0.0)
            flow = jnp.concatenate([jump * normal_ref[d:d + 1, at] for d in range(3)], axis=0)
            acc_ref[...] += joined(mm_nt(parts(flow), pm_ref[c]))
            return carry

        lax.fori_loop(0, chunks, gradient_step, 0)
        gradient = acc_ref[...] * inv_volume
        dsplit = parts(gradient)
        fill_payload(payg_ref, sec, joined(mm(dsplit, st_ref[...])))
        ghosts_start(gargs, sec)

        def reconstruct(c, carry):
            at = pl.ds(pl.multiple_of(c * chunk, chunk), chunk)
            left = joined(mm(dsplit, ot_ref[c]))
            right = joined(mm(dsplit, nt_ref[c, :cells]))
            tl, tr = left_ref[c], right_ref[c]
            for d in range(3):
                tl = tl + left[d * rows:(d + 1) * rows] * oarm_ref[d:d + 1, at]
                tr = tr + right[d * rows:(d + 1) * rows] * narm_ref[d:d + 1, at]
            left_ref[c] = tl
            right_ref[c] = tr
            return carry

        lax.fori_loop(0, chunks, reconstruct, 0)

        for k in range(1, ninst):
            peer_copy(sec, k).wait_recv()
        every = jnp.concatenate(
            [own_ref[sec]] + [peer_ref[sec, k - 1] for k in range(1, ninst)], axis=0
        )
        high = every.astype(BF).astype(F32)
        stacked = jnp.concatenate([every, every - high, every], axis=0).astype(BF)
        spectral = mm(table_ref[...], stacked)

        ghosts_wait(gargs, sec)
        hsplit = parts(ghost_values(gg_ref, sec))
        acc_ref[:rows] = jnp.zeros((rows, cells), F32)

        def flux_step(c, carry):
            at = pl.ds(pl.multiple_of(c * chunk, chunk), chunk)
            extra = joined(mm(hsplit, nt_ref[c, cells:]))
            tl, tr = left_ref[c], right_ref[c]
            for d in range(3):
                tr = tr + extra[d * rows:(d + 1) * rows] * narm_ref[d:d + 1, at]
            normals = [both_halves(normal_ref[d:d + 1, at]) for d in range(3)]
            area = jnp.sqrt(
                normals[0] * normals[0] + normals[1] * normals[1] + normals[2] * normals[2]
            )
            ul = [packed(tl, v) for v in range(nvar)]
            ur = [packed(tr, v) for v in range(nvar)]
            fl, sl = euler_flux(ul, normals, area)
            fr, sr = euler_flux(ur, normals, area)
            wave = jnp.maximum(sl, sr)
            flux = [
                0.5 * ((fl[v] + fr[v]) - wave * (ur[v] - ul[v])) for v in range(nvar)
            ] + [None]
            face = jnp.concatenate(
                [unpacked(flux[2 * j], flux[2 * j + 1]) for j in range((nvar + 1) // 2)], axis=0
            )
            live = (lane + c * chunk) < count_ref[...]
            face = jnp.where(live, face, 0.0)
            acc_ref[:rows] += joined(mm_nt(parts(face), dm_ref[c]))
            return carry

        lax.fori_loop(0, chunks, flux_step, 0)
        return acc_ref[:rows] * inv_volume + FREQUENCY * spectral

    step = step_ref[...]
    current = current - 0.5 * step * section(0, split)
    own_ref[1] = current
    for k in range(1, ninst):
        peer_copy(1, k).start()
    split = parts(current)
    fill_payload(payv_ref, 1, joined(mm(split, st_ref[...])))
    ghosts_start(vargs, 1)
    residual = section(1, split)
    new = own_ref[0] - step * residual
    for v in range(nvar):
        new_ref[v] = new[v * idev:(v + 1) * idev]
        res_ref[v] = residual[v * idev:(v + 1) * idev]

    for sec in range(2):
        ghosts_sent(vargs, sec)
        ghosts_sent(gargs, sec)
        for k in range(1, ninst):
            peer_copy(sec, k).wait_send()


def solution(mesh):
    ndom, ninst = mesh.shape["dom"], mesh.shape["inst"]

    def local(
        state, cell_volume, step_size, face_normal, owner_arm, neighbor_arm,
        face_owner, face_neighbor, face_count, send_cells,
    ):
        nvar, idev, cells = state.shape
        faces = face_owner.shape[0]
        slots = send_cells.shape[1]
        chunk = min(2048, faces)
        chunks = faces // chunk
        rows = -(-nvar * idev // 8) * 8
        ghosts = 4 * slots
        dims = (ndom, ninst, nvar, idev, cells, slots, chunks, chunk, rows)
        table = jnp.asarray(spectral_matrix(idev * ninst, idev, nvar, rows))
        vmem = pl.BlockSpec(memory_space=pltpu.VMEM)
        hbm = pl.BlockSpec(memory_space=pltpu.HBM)
        shape = jax.ShapeDtypeStruct(state.shape, F32)
        dma = pltpu.SemaphoreType.DMA
        return pl.pallas_call(
            functools.partial(kernel, dims),
            out_shape=(shape, shape),
            in_specs=[hbm] * 11,
            out_specs=(vmem, vmem),
            scratch_shapes=[
                pltpu.VMEM(state.shape, F32),
                pltpu.VMEM((1, cells), F32),
                pltpu.VMEM((1, cells), F32),
                pltpu.VMEM((3, faces), F32),
                pltpu.VMEM((3, faces), F32),
                pltpu.VMEM((3, faces), F32),
                pltpu.VMEM((1, faces), jnp.int32),
                pltpu.VMEM((1, faces), jnp.int32),
                pltpu.VMEM((1, 1), jnp.int32),
                pltpu.VMEM((4, slots), jnp.int32),
                pltpu.VMEM(table.shape, BF),
                dma((11,)),
                pltpu.VMEM((2, rows, cells), F32),
                pltpu.VMEM((2, ninst - 1, rows, cells), F32),
                pltpu.VMEM((2, 2, rows, 2 * slots), F32),
                pltpu.VMEM((2, 2, 3 * rows, 2 * slots), F32),
                pltpu.VMEM((2, 4, rows, 2 * slots), F32),
                pltpu.VMEM((2, 4, 3 * rows, 2 * slots), F32),
                pltpu.VMEM((cells, ghosts), BF),
                pltpu.VMEM((chunks, cells, chunk), BF),
                pltpu.VMEM((chunks, cells + ghosts, chunk), BF),
                pltpu.VMEM((chunks, cells, chunk), BF),
                pltpu.VMEM((chunks, cells, chunk), BF),
                pltpu.VMEM((chunks, rows, chunk), F32),
                pltpu.VMEM((chunks, rows, chunk), F32),
                pltpu.VMEM((3 * rows, cells), F32),
                dma((2, 4)), dma((2, 4)), dma((2, 4)), dma((2, 4)),
                dma((2, ninst - 1)), dma((2, ninst - 1)),
            ],
            compiler_params=pltpu.CompilerParams(
                collective_id=0, has_side_effects=True, vmem_limit_bytes=40 * 1024 * 1024
            ),
        )(*[
            x if x.size == 1 else pltpu.with_memory_space_constraint(x, pltpu.HBM)
            for x in (
                state, cell_volume[None], step_size[None], face_normal, owner_arm, neighbor_arm,
                face_owner[None], face_neighbor[None], face_count[None], send_cells, table,
            )
        ])

    placed = (
        P(None, "inst", "dom"),
        P("dom"),
        P("dom"),
        P(None, "dom"),
        P(None, "dom"),
        P(None, "dom"),
        P("dom"),
        P("dom"),
        P("dom"),
        P("dom", None),
    )
    return jax.shard_map(
        local,
        mesh=mesh,
        in_specs=placed,
        out_specs=(P(None, "inst", "dom"), P(None, "inst", "dom")),
        check_vma=False,
    )
```

```python
import functools

import jax
import jax.numpy as jnp
import numpy as np
from jax import lax
from jax.experimental import pallas as pl
from jax.experimental.pallas import tpu as pltpu
from jax.sharding import PartitionSpec as P

HEAT_RATIO = 1.4
FREQUENCY = 0.5
PEER_OFFSETS = (-2, -1, 1, 2)
MESH = pl.DeviceIdType.MESH
BF = jnp.bfloat16
F32 = jnp.float32


def spectral_matrix(points, inst_dev, nvar, rows):
    peers = points // inst_dev
    table = np.zeros((rows, peers * rows))
    for k in range(peers):
        for v in range(nvar):
            for t in range(inst_dev):
                for j in range(inst_dev):
                    d = (t - j - k * inst_dev) % points
                    if d:
                        table[v * inst_dev + t, k * rows + v * inst_dev + j] = (
                            0.5 * (-1.0) ** d / np.tan(np.pi * d / points)
                        )
    table = table.astype(np.float32)
    high = table.astype(jnp.bfloat16).astype(np.float32)
    low = table - high
    return np.concatenate([high, high, low], axis=1).astype(jnp.bfloat16)


def parts(x):
    high = x.astype(BF).astype(F32)
    return jnp.concatenate([x, x - high], axis=0).astype(BF)


def joined(y):
    half = y.shape[0] // 2
    return y[:half] + y[half:]


def mm(a, b):
    return lax.dot_general(a, b, (((1,), (0,)), ((), ())), preferred_element_type=F32)


def mm_nt(a, b):
    return lax.dot_general(a, b, (((1,), (1,)), ((), ())), preferred_element_type=F32)


def euler_flux(u, n, area):
    rho, m1, m2, m3, energy = u
    inv = 1.0 / rho
    u1, u2, u3 = m1 * inv, m2 * inv, m3 * inv
    pressure = (HEAT_RATIO - 1.0) * (energy - 0.5 * (m1 * u1 + m2 * u2 + m3 * u3))
    q = u1 * n[0] + u2 * n[1] + u3 * n[2]
    flux = (
        rho * q,
        m1 * q + pressure * n[0],
        m2 * q + pressure * n[1],
        m3 * q + pressure * n[2],
        (energy + pressure) * q,
    )
    speed = jnp.abs(q) + jnp.sqrt(HEAT_RATIO * pressure * inv) * area
    return flux, speed


def kernel(
    dims,
    state_hbm, volume_hbm, step_hbm, normal_hbm, oarm_hbm, narm_hbm, owner_hbm, neighbor_hbm,
    count_hbm, send_hbm, table_hbm,
    new_ref, res_ref,
    state_ref, volume_ref, step_ref, normal_ref, oarm_ref, narm_ref, owner_ref, neighbor_ref,
    count_ref, send_ref, table_ref, in_sem,
    own_ref, peer_ref, payv_ref, payg_ref, gv_ref, gg_ref,
    st_ref, ot_ref, nt_ref, pm_ref, dm_ref, left_ref, right_ref, acc_ref,
    sv_send, sv_recv, sg_send, sg_recv, sp_send, sp_recv,
):
    ndom, ninst, nvar, idev, cells, slots, chunks, chunk, rows = dims
    ghosts = 4 * slots
    me = lax.axis_index("dom")
    mi = lax.axis_index("inst")

    def valid(p):
        return (p >= 0) & (p < ndom)

    fetches = [
        pltpu.make_async_copy(source, target, in_sem.at[i])
        for i, (source, target) in enumerate((
            (state_hbm, state_ref), (send_hbm, send_ref),
            (owner_hbm, owner_ref), (neighbor_hbm, neighbor_ref),
            (volume_hbm, volume_ref), (count_hbm, count_ref), (normal_hbm, normal_ref),
            (oarm_hbm, oarm_ref), (narm_hbm, narm_ref),
            (step_hbm, step_ref), (table_hbm, table_ref),
        ))
    ]
    for fetch in fetches:
        fetch.start()
    gv_ref[...] = jnp.zeros(gv_ref.shape, F32)
    gg_ref[...] = jnp.zeros(gg_ref.shape, F32)

    barrier = pltpu.get_barrier_semaphore()
    for off in PEER_OFFSETS:
        @pl.when(valid(me + off))
        def _(off=off):
            pl.semaphore_signal(barrier, inc=1, device_id={"dom": me + off}, device_id_type=MESH)
    for k in range(1, ninst):
        pl.semaphore_signal(
            barrier, inc=1, device_id={"inst": lax.rem(mi + k, ninst)}, device_id_type=MESH
        )

    def ghost_copy(pay, dst, send, recv, sec, k, partition):
        return pltpu.make_async_remote_copy(
            src_ref=pay.at[sec, k],
            dst_ref=dst.at[sec, k],
            send_sem=send.at[sec, k],
            recv_sem=recv.at[sec, k],
            device_id={"dom": partition},
            device_id_type=MESH,
        )

    def ghosts_start(args, sec):
        for k, off in enumerate(PEER_OFFSETS):
            @pl.when(valid(me - off))
            def _(k=k, off=off):
                ghost_copy(*args, sec, k, me - off).start()

    def ghosts_wait(args, sec):
        for k, off in enumerate(PEER_OFFSETS):
            @pl.when(valid(me + off))
            def _(k=k, off=off):
                ghost_copy(*args, sec, k, me + off).wait_recv()

    def ghosts_sent(args, sec):
        for k, off in enumerate(PEER_OFFSETS):
            @pl.when(valid(me - off))
            def _(k=k, off=off):
                ghost_copy(*args, sec, k, me - off).wait_send()

    def peer_copy(sec, k):
        return pltpu.make_async_remote_copy(
            src_ref=own_ref.at[sec],
            dst_ref=peer_ref.at[sec, k - 1],
            send_sem=sp_send.at[sec, k - 1],
            recv_sem=sp_recv.at[sec, k - 1],
            device_id={"inst": lax.rem(mi + ninst - k, ninst)},
            device_id_type=MESH,
        )

    vargs = (payv_ref, gv_ref, sv_send, sv_recv)
    gargs = (payg_ref, gg_ref, sg_send, sg_recv)

    for fetch in fetches[:2]:
        fetch.wait()
    cell_id = lax.broadcasted_iota(jnp.int32, (cells, slots), 0)
    for k in range(4):
        hit = cell_id == send_ref[k:k + 1, :]
        st_ref[:, k * slots:(k + 1) * slots] = jnp.where(hit, 1.0, 0.0).astype(BF)

    pad = rows - nvar * idev
    filler = [jnp.zeros((pad, cells), F32)] if pad else []
    current = jnp.concatenate([state_ref[v] for v in range(nvar)] + filler, axis=0)
    own_ref[0] = current
    split = parts(current)

    def fill_payload(pay, sec, values):
        high = pay.shape[2]
        first = lax.broadcasted_iota(jnp.int32, (high, 2 * slots), 1) < slots
        for j in range(2):
            pair = values[:, j * 2 * slots:(j + 1) * 2 * slots]
            top, bottom = pair[:high], pair[pair.shape[0] - high:]
            pay[sec, 2 * j] = jnp.where(first, top, pltpu.roll(bottom, slots, 1))
            pay[sec, 2 * j + 1] = jnp.where(first, pltpu.roll(top, slots, 1), bottom)

    fill_payload(payv_ref, 0, joined(mm(split, st_ref[...])))

    neighbours = sum(valid(me + off).astype(jnp.int32) for off in PEER_OFFSETS)
    pl.semaphore_wait(barrier, neighbours + (ninst - 1))

    ghosts_start(vargs, 0)
    for k in range(1, ninst):
        peer_copy(0, k).start()

    for fetch in fetches[2:]:
        fetch.wait()
    def build(c, carry):
        at = pl.ds(pl.multiple_of(c * chunk, chunk), chunk)
        ids = lax.broadcasted_iota(jnp.int32, (cells, chunk), 0)
        gids = lax.broadcasted_iota(jnp.int32, (ghosts, chunk), 0) + cells
        own = owner_ref[:, at]
        nbr = neighbor_ref[:, at]
        o = jnp.where(ids == own, 1.0, 0.0).astype(BF)
        n = jnp.where(ids == nbr, 1.0, 0.0).astype(BF)
        ot_ref[c] = o
        nt_ref[c, :cells] = n
        nt_ref[c, cells:] = jnp.where(gids == nbr, 1.0, 0.0).astype(BF)
        pm_ref[c] = o + n
        dm_ref[c] = o - n
        return carry

    lax.fori_loop(0, chunks, build, 0)

    inv_volume = 1.0 / volume_ref[...]
    lane = lax.broadcasted_iota(jnp.int32, (1, chunk), 1)
    half = chunk // 2
    low_rows = lax.broadcasted_iota(jnp.int32, (2 * idev, half), 0) < idev

    def packed(x, v):
        tile = x[(v // 2) * 2 * idev:(v // 2 + 1) * 2 * idev]
        a, b = tile[:, :half], tile[:, half:]
        if v % 2 == 0:
            return jnp.where(low_rows, a, pltpu.roll(b, idev, 0))
        return jnp.where(low_rows, pltpu.roll(a, idev, 0), b)

    def unpacked(even, odd):
        if odd is None:
            a = jnp.where(low_rows, even, 0.0)
            b = jnp.where(low_rows, pltpu.roll(even, idev, 0), 0.0)
        else:
            a = jnp.where(low_rows, even, pltpu.roll(odd, idev, 0))
            b = jnp.where(low_rows, pltpu.roll(even, idev, 0), odd)
        return jnp.concatenate([a, b], axis=1)

    def both_halves(x):
        return jnp.where(low_rows, x[:, :half], x[:, half:])

    def ghost_values(ref, sec, wide):
        high = ref.shape[2]
        first = lax.broadcasted_iota(jnp.int32, (high, 2 * slots), 1) < slots
        pairs = []
        for j in range(2):
            a, b = ref[sec, 2 * j], ref[sec, 2 * j + 1]
            top = jnp.where(first, a, pltpu.roll(b, slots, 1))
            bottom = jnp.where(first, pltpu.roll(a, slots, 1), b)
            pairs.append(jnp.concatenate([top, bottom[2 * high - wide:]], axis=0))
        return jnp.concatenate(pairs, axis=1)

    def section(sec, split):
        def gather_local(c, carry):
            left_ref[c] = joined(mm(split, ot_ref[c]))
            right_ref[c] = joined(mm(split, nt_ref[c, :cells]))
            return carry

        lax.fori_loop(0, chunks, gather_local, 0)
        ghosts_wait(vargs, sec)
        gsplit = parts(ghost_values(gv_ref, sec, rows))
        acc_ref[...] = jnp.zeros(acc_ref.shape, F32)

        def gradient_step(c, carry):
            at = pl.ds(pl.multiple_of(c * chunk, chunk), chunk)
            right = right_ref[c] + joined(mm(gsplit, nt_ref[c, cells:]))
            right_ref[c] = right
            live = (lane + c * chunk) < count_ref[...]
            jump = jnp.where(live, 0.5 * (right - left_ref[c]), 0.0)
            flow = jnp.concatenate([jump * normal_ref[d:d + 1, at] for d in range(3)], axis=0)
            acc_ref[...] += joined(mm_nt(parts(flow), pm_ref[c]))
            return carry

        lax.fori_loop(0, chunks, gradient_step, 0)
        gradient = acc_ref[...] * inv_volume
        dsplit = parts(gradient)
        fill_payload(payg_ref, sec, joined(mm(dsplit, st_ref[...])))
        ghosts_start(gargs, sec)

        def reconstruct(c, carry):
            at = pl.ds(pl.multiple_of(c * chunk, chunk), chunk)
            left = joined(mm(dsplit, ot_ref[c]))
            right = joined(mm(dsplit, nt_ref[c, :cells]))
            tl, tr = left_ref[c], right_ref[c]
            for d in range(3):
                tl = tl + left[d * rows:(d + 1) * rows] * oarm_ref[d:d + 1, at]
                tr = tr + right[d * rows:(d + 1) * rows] * narm_ref[d:d + 1, at]
            left_ref[c] = tl
            right_ref[c] = tr
            return carry

        lax.fori_loop(0, chunks, reconstruct, 0)

        for k in range(1, ninst):
            peer_copy(sec, k).wait_recv()
        every = jnp.concatenate(
            [own_ref[sec]] + [peer_ref[sec, k - 1] for k in range(1, ninst)], axis=0
        )
        high = every.astype(BF).astype(F32)
        stacked = jnp.concatenate([every, every - high, every], axis=0).astype(BF)
        spectral = mm(table_ref[...], stacked)

        ghosts_wait(gargs, sec)
        hsplit = parts(ghost_values(gg_ref, sec, 3 * rows))
        acc_ref[:rows] = jnp.zeros((rows, cells), F32)

        def flux_step(c, carry):
            at = pl.ds(pl.multiple_of(c * chunk, chunk), chunk)
            extra = joined(mm(hsplit, nt_ref[c, cells:]))
            tl, tr = left_ref[c], right_ref[c]
            for d in range(3):
                tr = tr + extra[d * rows:(d + 1) * rows] * narm_ref[d:d + 1, at]
            normals = [both_halves(normal_ref[d:d + 1, at]) for d in range(3)]
            area = jnp.sqrt(
                normals[0] * normals[0] + normals[1] * normals[1] + normals[2] * normals[2]
            )
            ul = [packed(tl, v) for v in range(nvar)]
            ur = [packed(tr, v) for v in range(nvar)]
            fl, sl = euler_flux(ul, normals, area)
            fr, sr = euler_flux(ur, normals, area)
            wave = jnp.maximum(sl, sr)
            flux = [
                0.5 * ((fl[v] + fr[v]) - wave * (ur[v] - ul[v])) for v in range(nvar)
            ] + [None]
            face = jnp.concatenate(
                [unpacked(flux[2 * j], flux[2 * j + 1]) for j in range((nvar + 1) // 2)], axis=0
            )
            live = (lane + c * chunk) < count_ref[...]
            face = jnp.where(live, face, 0.0)
            acc_ref[:rows] += joined(mm_nt(parts(face), dm_ref[c]))
            return carry

        lax.fori_loop(0, chunks, flux_step, 0)
        return acc_ref[:rows] * inv_volume + FREQUENCY * spectral

    step = step_ref[...]
    current = current - 0.5 * step * section(0, split)
    own_ref[1] = current
    split = parts(current)
    fill_payload(payv_ref, 1, joined(mm(split, st_ref[...])))
    ghosts_start(vargs, 1)
    for k in range(1, ninst):
        peer_copy(1, k).start()
    residual = section(1, split)
    new = own_ref[0] - step * residual
    for v in range(nvar):
        new_ref[v] = new[v * idev:(v + 1) * idev]
        res_ref[v] = residual[v * idev:(v + 1) * idev]

    for sec in range(2):
        ghosts_sent(vargs, sec)
        ghosts_sent(gargs, sec)
        for k in range(1, ninst):
            peer_copy(sec, k).wait_send()


def leave(new_ref, res_ref, new_out, res_out, sems):
    copies = [
        pltpu.make_async_copy(new_ref, new_out, sems.at[0]),
        pltpu.make_async_copy(res_ref, res_out, sems.at[1]),
    ]
    for copy in copies:
        copy.start()
    for copy in copies:
        copy.wait()


def solution(mesh):
    ndom, ninst = mesh.shape["dom"], mesh.shape["inst"]

    def local(
        state, cell_volume, step_size, face_normal, owner_arm, neighbor_arm,
        face_owner, face_neighbor, face_count, send_cells,
    ):
        nvar, idev, cells = state.shape
        faces = face_owner.shape[0]
        slots = send_cells.shape[1]
        chunk = min(2048, faces)
        chunks = faces // chunk
        rows = -(-nvar * idev // 8) * 8
        ghosts = 4 * slots
        vhigh = -(-rows // 16) * 8
        ghigh = -(-3 * rows // 16) * 8
        dims = (ndom, ninst, nvar, idev, cells, slots, chunks, chunk, rows)
        table = jnp.asarray(spectral_matrix(idev * ninst, idev, nvar, rows))
        vmem = pl.BlockSpec(memory_space=pltpu.VMEM)
        hbm = pl.BlockSpec(memory_space=pltpu.HBM)
        shape = jax.ShapeDtypeStruct(state.shape, F32)
        dma = pltpu.SemaphoreType.DMA
        results = pl.pallas_call(
            functools.partial(kernel, dims),
            out_shape=(shape, shape),
            in_specs=[hbm] * 11,
            out_specs=(vmem, vmem),
            scratch_shapes=[
                pltpu.VMEM(state.shape, F32),
                pltpu.VMEM((1, cells), F32),
                pltpu.VMEM((1, cells), F32),
                pltpu.VMEM((3, faces), F32),
                pltpu.VMEM((3, faces), F32),
                pltpu.VMEM((3, faces), F32),
                pltpu.VMEM((1, faces), jnp.int32),
                pltpu.VMEM((1, faces), jnp.int32),
                pltpu.VMEM((1, 1), jnp.int32),
                pltpu.VMEM((4, slots), jnp.int32),
                pltpu.VMEM(table.shape, BF),
                dma((11,)),
                pltpu.VMEM((2, rows, cells), F32),
                pltpu.VMEM((2, ninst - 1, rows, cells), F32),
                pltpu.VMEM((2, 4, vhigh, 2 * slots), F32),
                pltpu.VMEM((2, 4, ghigh, 2 * slots), F32),
                pltpu.VMEM((2, 4, vhigh, 2 * slots), F32),
                pltpu.VMEM((2, 4, ghigh, 2 * slots), F32),
                pltpu.VMEM((cells, ghosts), BF),
                pltpu.VMEM((chunks, cells, chunk), BF),
                pltpu.VMEM((chunks, cells + ghosts, chunk), BF),
                pltpu.VMEM((chunks, cells, chunk), BF),
                pltpu.VMEM((chunks, cells, chunk), BF),
                pltpu.VMEM((chunks, rows, chunk), F32),
                pltpu.VMEM((chunks, rows, chunk), F32),
                pltpu.VMEM((3 * rows, cells), F32),
                dma((2, 4)), dma((2, 4)), dma((2, 4)), dma((2, 4)),
                dma((2, ninst - 1)), dma((2, ninst - 1)),
            ],
            compiler_params=pltpu.CompilerParams(
                collective_id=0, has_side_effects=True, vmem_limit_bytes=40 * 1024 * 1024
            ),
        )(*[
            x if x.size == 1 else pltpu.with_memory_space_constraint(x, pltpu.HBM)
            for x in (
                state, cell_volume[None], step_size[None], face_normal, owner_arm, neighbor_arm,
                face_owner[None], face_neighbor[None], face_count[None], send_cells, table,
            )
        ])
        return pl.pallas_call(
            leave,
            out_shape=(shape, shape),
            in_specs=[vmem, vmem],
            out_specs=(hbm, hbm),
            scratch_shapes=[dma((2,))],
        )(*results)

    placed = (
        P(None, "inst", "dom"),
        P("dom"),
        P("dom"),
        P(None, "dom"),
        P(None, "dom"),
        P(None, "dom"),
        P("dom"),
        P("dom"),
        P("dom"),
        P("dom", None),
    )
    return jax.shard_map(
        local,
        mesh=mesh,
        in_specs=placed,
        out_specs=(P(None, "inst", "dom"), P(None, "inst", "dom")),
        check_vma=False,
    )
```

```python
import functools

import jax
import jax.numpy as jnp
import numpy as np
from jax import lax
from jax.experimental import pallas as pl
from jax.experimental.pallas import tpu as pltpu
from jax.sharding import PartitionSpec as P

HEAT_RATIO = 1.4
FREQUENCY = 0.5
PEER_OFFSETS = (-2, -1, 1, 2)
MESH = pl.DeviceIdType.MESH
BF = jnp.bfloat16
F32 = jnp.float32


def spectral_matrix(points, inst_dev, nvar, rows):
    peers = points // inst_dev
    table = np.zeros((rows, peers * rows))
    for k in range(peers):
        for v in range(nvar):
            for t in range(inst_dev):
                for j in range(inst_dev):
                    d = (t - j - k * inst_dev) % points
                    if d:
                        table[v * inst_dev + t, k * rows + v * inst_dev + j] = (
                            0.5 * (-1.0) ** d / np.tan(np.pi * d / points)
                        )
    table = table.astype(np.float32)
    high = table.astype(jnp.bfloat16).astype(np.float32)
    low = table - high
    return np.concatenate([high, high, low], axis=1).astype(jnp.bfloat16)


def parts(x):
    high = x.astype(BF).astype(F32)
    return jnp.concatenate([x, x - high], axis=0).astype(BF)


def joined(y):
    half = y.shape[0] // 2
    return y[:half] + y[half:]


def mm(a, b):
    return lax.dot_general(a, b, (((1,), (0,)), ((), ())), preferred_element_type=F32)


def mm_nt(a, b):
    return lax.dot_general(a, b, (((1,), (1,)), ((), ())), preferred_element_type=F32)


def euler_flux(u, n, area):
    rho, m1, m2, m3, energy = u
    inv = 1.0 / rho
    u1, u2, u3 = m1 * inv, m2 * inv, m3 * inv
    pressure = (HEAT_RATIO - 1.0) * (energy - 0.5 * (m1 * u1 + m2 * u2 + m3 * u3))
    q = u1 * n[0] + u2 * n[1] + u3 * n[2]
    flux = (
        rho * q,
        m1 * q + pressure * n[0],
        m2 * q + pressure * n[1],
        m3 * q + pressure * n[2],
        (energy + pressure) * q,
    )
    speed = jnp.abs(q) + jnp.sqrt(HEAT_RATIO * pressure * inv) * area
    return flux, speed


def kernel(
    dims,
    state_hbm, volume_hbm, step_hbm, normal_hbm, oarm_hbm, narm_hbm, owner_hbm, neighbor_hbm,
    count_ref, send_hbm, table_hbm,
    new_ref, res_ref,
    state_ref, volume_ref, step_ref, normal_ref, oarm_ref, narm_ref, owner_ref, neighbor_ref,
    send_ref, table_ref, in_sem,
    own_ref, peer_ref, payv_ref, payg_ref, gv_ref, gg_ref,
    st_ref, ot_ref, nt_ref, pm_ref, dm_ref, left_ref, right_ref, acc_ref,
    sv_send, sv_recv, sg_send, sg_recv, sp_send, sp_recv,
):
    ndom, ninst, nvar, idev, cells, slots, chunks, chunk, rows = dims
    ghosts = 4 * slots
    me = lax.axis_index("dom")
    mi = lax.axis_index("inst")

    def valid(p):
        return (p >= 0) & (p < ndom)

    fetches = [
        pltpu.make_async_copy(source, target, in_sem.at[i])
        for i, (source, target) in enumerate((
            (state_hbm, state_ref), (send_hbm, send_ref),
            (owner_hbm, owner_ref), (neighbor_hbm, neighbor_ref),
            (volume_hbm, volume_ref), (normal_hbm, normal_ref),
            (oarm_hbm, oarm_ref), (narm_hbm, narm_ref),
            (step_hbm, step_ref), (table_hbm, table_ref),
        ))
    ]
    for fetch in fetches:
        fetch.start()
    gv_ref[...] = jnp.zeros(gv_ref.shape, F32)
    gg_ref[...] = jnp.zeros(gg_ref.shape, F32)

    barrier = pltpu.get_barrier_semaphore()
    for off in PEER_OFFSETS:
        @pl.when(valid(me + off))
        def _(off=off):
            pl.semaphore_signal(barrier, inc=1, device_id={"dom": me + off}, device_id_type=MESH)
    for k in range(1, ninst):
        pl.semaphore_signal(
            barrier, inc=1, device_id={"inst": lax.rem(mi + k, ninst)}, device_id_type=MESH
        )

    def ghost_copy(pay, dst, send, recv, sec, k, partition):
        return pltpu.make_async_remote_copy(
            src_ref=pay.at[sec, k],
            dst_ref=dst.at[sec, k],
            send_sem=send.at[sec, k],
            recv_sem=recv.at[sec, k],
            device_id={"dom": partition},
            device_id_type=MESH,
        )

    def ghosts_start(args, sec):
        for k, off in enumerate(PEER_OFFSETS):
            @pl.when(valid(me - off))
            def _(k=k, off=off):
                ghost_copy(*args, sec, k, me - off).start()

    def ghosts_wait(args, sec):
        for k, off in enumerate(PEER_OFFSETS):
            @pl.when(valid(me + off))
            def _(k=k, off=off):
                ghost_copy(*args, sec, k, me + off).wait_recv()

    def ghosts_sent(args, sec):
        for k, off in enumerate(PEER_OFFSETS):
            @pl.when(valid(me - off))
            def _(k=k, off=off):
                ghost_copy(*args, sec, k, me - off).wait_send()

    def peer_copy(sec, k):
        return pltpu.make_async_remote_copy(
            src_ref=own_ref.at[sec],
            dst_ref=peer_ref.at[sec, k - 1],
            send_sem=sp_send.at[sec, k - 1],
            recv_sem=sp_recv.at[sec, k - 1],
            device_id={"inst": lax.rem(mi + ninst - k, ninst)},
            device_id_type=MESH,
        )

    vargs = (payv_ref, gv_ref, sv_send, sv_recv)
    gargs = (payg_ref, gg_ref, sg_send, sg_recv)

    for fetch in fetches[:2]:
        fetch.wait()
    cell_id = lax.broadcasted_iota(jnp.int32, (cells, slots), 0)
    for k in range(4):
        hit = cell_id == send_ref[k:k + 1, :]
        st_ref[:, k * slots:(k + 1) * slots] = jnp.where(hit, 1.0, 0.0).astype(BF)

    pad = rows - nvar * idev
    filler = [jnp.zeros((pad, cells), F32)] if pad else []
    current = jnp.concatenate([state_ref[v] for v in range(nvar)] + filler, axis=0)
    own_ref[0] = current
    split = parts(current)

    def fill_payload(pay, sec, values):
        high = pay.shape[2]
        first = lax.broadcasted_iota(jnp.int32, (high, 2 * slots), 1) < slots
        for j in range(2):
            pair = values[:, j * 2 * slots:(j + 1) * 2 * slots]
            top, bottom = pair[:high], pair[pair.shape[0] - high:]
            pay[sec, 2 * j] = jnp.where(first, top, pltpu.roll(bottom, slots, 1))
            pay[sec, 2 * j + 1] = jnp.where(first, pltpu.roll(top, slots, 1), bottom)

    fill_payload(payv_ref, 0, joined(mm(split, st_ref[...])))

    neighbours = sum(valid(me + off).astype(jnp.int32) for off in PEER_OFFSETS)
    pl.semaphore_wait(barrier, neighbours + (ninst - 1))

    ghosts_start(vargs, 0)
    for k in range(1, ninst):
        peer_copy(0, k).start()

    for fetch in fetches[2:]:
        fetch.wait()
    def build(c, carry):
        at = pl.ds(pl.multiple_of(c * chunk, chunk), chunk)
        ids = lax.broadcasted_iota(jnp.int16, (cells + ghosts, chunk), 0)
        one, zero = jnp.ones((), BF), jnp.zeros((), BF)
        own = owner_ref[:, at].astype(jnp.int16)
        nbr = neighbor_ref[:, at].astype(jnp.int16)
        ot_ref[c] = jnp.where(ids[:cells] == own, one, zero)
        nt_ref[c] = jnp.where(ids == nbr, one, zero)
        return carry

    def build_sum(c, carry):
        pm_ref[c] = ot_ref[c] + nt_ref[c, :cells]
        return carry

    def build_difference(c, carry):
        dm_ref[c] = ot_ref[c] - nt_ref[c, :cells]
        return carry

    lax.fori_loop(0, chunks, build, 0)

    inv_volume = 1.0 / volume_ref[...]
    lane = lax.broadcasted_iota(jnp.int32, (1, chunk), 1)
    half = chunk // 2
    low_rows = lax.broadcasted_iota(jnp.int32, (2 * idev, half), 0) < idev

    def packed(x, v):
        tile = x[(v // 2) * 2 * idev:(v // 2 + 1) * 2 * idev]
        a, b = tile[:, :half], tile[:, half:]
        if v % 2 == 0:
            return jnp.where(low_rows, a, pltpu.roll(b, idev, 0))
        return jnp.where(low_rows, pltpu.roll(a, idev, 0), b)

    def unpacked(even, odd):
        if odd is None:
            a = jnp.where(low_rows, even, 0.0)
            b = jnp.where(low_rows, pltpu.roll(even, idev, 0), 0.0)
        else:
            a = jnp.where(low_rows, even, pltpu.roll(odd, idev, 0))
            b = jnp.where(low_rows, pltpu.roll(even, idev, 0), odd)
        return jnp.concatenate([a, b], axis=1)

    def both_halves(x):
        return jnp.where(low_rows, x[:, :half], x[:, half:])

    def ghost_values(ref, sec, wide):
        high = ref.shape[2]
        first = lax.broadcasted_iota(jnp.int32, (high, 2 * slots), 1) < slots
        pairs = []
        for j in range(2):
            a, b = ref[sec, 2 * j], ref[sec, 2 * j + 1]
            top = jnp.where(first, a, pltpu.roll(b, slots, 1))
            bottom = jnp.where(first, pltpu.roll(a, slots, 1), b)
            pairs.append(jnp.concatenate([top, bottom[2 * high - wide:]], axis=0))
        return jnp.concatenate(pairs, axis=1)

    def section(sec, split):
        def gather_local(c, carry):
            left_ref[c] = joined(mm(split, ot_ref[c]))
            right_ref[c] = joined(mm(split, nt_ref[c, :cells]))
            return carry

        lax.fori_loop(0, chunks, gather_local, 0)
        if sec == 0:
            lax.fori_loop(0, chunks, build_sum, 0)
        ghosts_wait(vargs, sec)
        gsplit = parts(ghost_values(gv_ref, sec, rows))
        acc_ref[...] = jnp.zeros(acc_ref.shape, F32)

        def gradient_step(c, carry):
            at = pl.ds(pl.multiple_of(c * chunk, chunk), chunk)
            right = right_ref[c] + joined(mm(gsplit, nt_ref[c, cells:]))
            right_ref[c] = right
            live = (lane + c * chunk) < count_ref[0]
            jump = jnp.where(live, 0.5 * (right - left_ref[c]), 0.0)
            flow = jnp.concatenate([jump * normal_ref[d:d + 1, at] for d in range(3)], axis=0)
            acc_ref[...] += joined(mm_nt(parts(flow), pm_ref[c]))
            return carry

        lax.fori_loop(0, chunks, gradient_step, 0)
        gradient = acc_ref[...] * inv_volume
        dsplit = parts(gradient)
        fill_payload(payg_ref, sec, joined(mm(dsplit, st_ref[...])))
        ghosts_start(gargs, sec)

        def reconstruct(c, carry):
            at = pl.ds(pl.multiple_of(c * chunk, chunk), chunk)
            left = joined(mm(dsplit, ot_ref[c]))
            right = joined(mm(dsplit, nt_ref[c, :cells]))
            tl, tr = left_ref[c], right_ref[c]
            for d in range(3):
                tl = tl + left[d * rows:(d + 1) * rows] * oarm_ref[d:d + 1, at]
                tr = tr + right[d * rows:(d + 1) * rows] * narm_ref[d:d + 1, at]
            left_ref[c] = tl
            right_ref[c] = tr
            return carry

        lax.fori_loop(0, chunks, reconstruct, 0)
        if sec == 0:
            lax.fori_loop(0, chunks, build_difference, 0)

        for k in range(1, ninst):
            peer_copy(sec, k).wait_recv()
        every = jnp.concatenate(
            [own_ref[sec]] + [peer_ref[sec, k - 1] for k in range(1, ninst)], axis=0
        )
        high = every.astype(BF).astype(F32)
        stacked = jnp.concatenate([every, every - high, every], axis=0).astype(BF)
        spectral = mm(table_ref[...], stacked)

        ghosts_wait(gargs, sec)
        hsplit = parts(ghost_values(gg_ref, sec, 3 * rows))
        acc_ref[:rows] = jnp.zeros((rows, cells), F32)

        def flux_step(c, carry):
            at = pl.ds(pl.multiple_of(c * chunk, chunk), chunk)
            extra = joined(mm(hsplit, nt_ref[c, cells:]))
            tl, tr = left_ref[c], right_ref[c]
            for d in range(3):
                tr = tr + extra[d * rows:(d + 1) * rows] * narm_ref[d:d + 1, at]
            normals = [both_halves(normal_ref[d:d + 1, at]) for d in range(3)]
            area = jnp.sqrt(
                normals[0] * normals[0] + normals[1] * normals[1] + normals[2] * normals[2]
            )
            ul = [packed(tl, v) for v in range(nvar)]
            ur = [packed(tr, v) for v in range(nvar)]
            fl, sl = euler_flux(ul, normals, area)
            fr, sr = euler_flux(ur, normals, area)
            wave = jnp.maximum(sl, sr)
            flux = [
                0.5 * ((fl[v] + fr[v]) - wave * (ur[v] - ul[v])) for v in range(nvar)
            ] + [None]
            face = jnp.concatenate(
                [unpacked(flux[2 * j], flux[2 * j + 1]) for j in range((nvar + 1) // 2)], axis=0
            )
            live = (lane + c * chunk) < count_ref[0]
            face = jnp.where(live, face, 0.0)
            acc_ref[:rows] += joined(mm_nt(parts(face), dm_ref[c]))
            return carry

        lax.fori_loop(0, chunks, flux_step, 0)
        return acc_ref[:rows] * inv_volume + FREQUENCY * spectral

    step = step_ref[...]
    current = current - 0.5 * step * section(0, split)
    own_ref[1] = current
    split = parts(current)
    fill_payload(payv_ref, 1, joined(mm(split, st_ref[...])))
    ghosts_start(vargs, 1)
    for k in range(1, ninst):
        peer_copy(1, k).start()
    residual = section(1, split)
    new = own_ref[0] - step * residual
    for v in range(nvar):
        new_ref[v] = new[v * idev:(v + 1) * idev]
        res_ref[v] = residual[v * idev:(v + 1) * idev]

    for sec in range(2):
        ghosts_sent(vargs, sec)
        ghosts_sent(gargs, sec)
        for k in range(1, ninst):
            peer_copy(sec, k).wait_send()


def solution(mesh):
    ndom, ninst = mesh.shape["dom"], mesh.shape["inst"]

    def local(
        state, cell_volume, step_size, face_normal, owner_arm, neighbor_arm,
        face_owner, face_neighbor, face_count, send_cells,
    ):
        nvar, idev, cells = state.shape
        faces = face_owner.shape[0]
        slots = send_cells.shape[1]
        chunk = min(2048, faces)
        chunks = faces // chunk
        rows = -(-nvar * idev // 8) * 8
        ghosts = 4 * slots
        vhigh = -(-rows // 16) * 8
        ghigh = -(-3 * rows // 16) * 8
        dims = (ndom, ninst, nvar, idev, cells, slots, chunks, chunk, rows)
        table = jnp.asarray(spectral_matrix(idev * ninst, idev, nvar, rows))
        vmem = pl.BlockSpec(memory_space=pltpu.VMEM)
        hbm = pl.BlockSpec(memory_space=pltpu.HBM)
        shape = jax.ShapeDtypeStruct(state.shape, F32)
        dma = pltpu.SemaphoreType.DMA
        return pl.pallas_call(
            functools.partial(kernel, dims),
            out_shape=(shape, shape),
            in_specs=[hbm] * 8 + [pl.BlockSpec(memory_space=pltpu.SMEM)] + [hbm] * 2,
            out_specs=(vmem, vmem),
            scratch_shapes=[
                pltpu.VMEM(state.shape, F32),
                pltpu.VMEM((1, cells), F32),
                pltpu.VMEM((1, cells), F32),
                pltpu.VMEM((3, faces), F32),
                pltpu.VMEM((3, faces), F32),
                pltpu.VMEM((3, faces), F32),
                pltpu.VMEM((1, faces), jnp.int32),
                pltpu.VMEM((1, faces), jnp.int32),
                pltpu.VMEM((4, slots), jnp.int32),
                pltpu.VMEM(table.shape, BF),
                dma((10,)),
                pltpu.VMEM((2, rows, cells), F32),
                pltpu.VMEM((2, ninst - 1, rows, cells), F32),
                pltpu.VMEM((2, 4, vhigh, 2 * slots), F32),
                pltpu.VMEM((2, 4, ghigh, 2 * slots), F32),
                pltpu.VMEM((2, 4, vhigh, 2 * slots), F32),
                pltpu.VMEM((2, 4, ghigh, 2 * slots), F32),
                pltpu.VMEM((cells, ghosts), BF),
                pltpu.VMEM((chunks, cells, chunk), BF),
                pltpu.VMEM((chunks, cells + ghosts, chunk), BF),
                pltpu.VMEM((chunks, cells, chunk), BF),
                pltpu.VMEM((chunks, cells, chunk), BF),
                pltpu.VMEM((chunks, rows, chunk), F32),
                pltpu.VMEM((chunks, rows, chunk), F32),
                pltpu.VMEM((3 * rows, cells), F32),
                dma((2, 4)), dma((2, 4)), dma((2, 4)), dma((2, 4)),
                dma((2, ninst - 1)), dma((2, ninst - 1)),
            ],
            compiler_params=pltpu.CompilerParams(
                collective_id=0, has_side_effects=True, vmem_limit_bytes=40 * 1024 * 1024
            ),
        )(*[
            x if x.size == 1 else pltpu.with_memory_space_constraint(x, pltpu.HBM)
            for x in (
                state, cell_volume[None], step_size[None], face_normal, owner_arm, neighbor_arm,
                face_owner[None], face_neighbor[None], face_count, send_cells, table,
            )
        ])

    placed = (
        P(None, "inst", "dom"),
        P("dom"),
        P("dom"),
        P(None, "dom"),
        P(None, "dom"),
        P(None, "dom"),
        P("dom"),
        P("dom"),
        P("dom"),
        P("dom", None),
    )
    return jax.shard_map(
        local,
        mesh=mesh,
        in_specs=placed,
        out_specs=(P(None, "inst", "dom"), P(None, "inst", "dom")),
        check_vma=False,
    )
```

```python
import functools

import jax
import jax.numpy as jnp
import numpy as np
from jax import lax
from jax.experimental import pallas as pl
from jax.experimental.pallas import tpu as pltpu
from jax.sharding import PartitionSpec as P

HEAT_RATIO = 1.4
FREQUENCY = 0.5
PEER_OFFSETS = (-2, -1, 1, 2)
MESH = pl.DeviceIdType.MESH
BF = jnp.bfloat16
F32 = jnp.float32


def spectral_matrix(points, inst_dev, nvar, rows):
    peers = points // inst_dev
    table = np.zeros((rows, peers * rows))
    for k in range(peers):
        for v in range(nvar):
            for t in range(inst_dev):
                for j in range(inst_dev):
                    d = (t - j - k * inst_dev) % points
                    if d:
                        table[v * inst_dev + t, k * rows + v * inst_dev + j] = (
                            0.5 * (-1.0) ** d / np.tan(np.pi * d / points)
                        )
    table = table.astype(np.float32)
    high = table.astype(jnp.bfloat16).astype(np.float32)
    low = table - high
    return np.concatenate([high, high, low], axis=1).astype(jnp.bfloat16)


def parts(x):
    high = x.astype(BF).astype(F32)
    return jnp.concatenate([x, x - high], axis=0).astype(BF)


def joined(y):
    half = y.shape[0] // 2
    return y[:half] + y[half:]


def mm(a, b):
    return lax.dot_general(a, b, (((1,), (0,)), ((), ())), preferred_element_type=F32)


def euler_flux(u, n, area):
    rho, m1, m2, m3, energy = u
    inv = 1.0 / rho
    u1, u2, u3 = m1 * inv, m2 * inv, m3 * inv
    pressure = (HEAT_RATIO - 1.0) * (energy - 0.5 * (m1 * u1 + m2 * u2 + m3 * u3))
    q = u1 * n[0] + u2 * n[1] + u3 * n[2]
    flux = (
        rho * q,
        m1 * q + pressure * n[0],
        m2 * q + pressure * n[1],
        m3 * q + pressure * n[2],
        (energy + pressure) * q,
    )
    speed = jnp.abs(q) + jnp.sqrt(HEAT_RATIO * pressure * inv) * area
    return flux, speed


def kernel(
    dims,
    state_hbm, volume_hbm, step_hbm, normal_hbm, oarm_hbm, narm_hbm, owner_hbm, neighbor_hbm,
    count_ref, send_hbm, table_hbm,
    new_ref, res_ref,
    state_ref, volume_ref, step_ref, normal_ref, oarm_ref, narm_ref, owner_ref, neighbor_ref,
    send_ref, table_ref, in_sem,
    own_ref, peer_ref, payv_ref, payg_ref, gv_ref, gg_ref,
    st_ref, ot_ref, nt_ref, pm_ref, dm_ref, left_ref, right_ref, acc_ref,
    sv_send, sv_recv, sg_send, sg_recv, sp_send, sp_recv,
):
    ndom, ninst, nvar, idev, cells, slots, chunks, chunk, rows = dims
    ghosts = 4 * slots
    me = lax.axis_index("dom")
    mi = lax.axis_index("inst")

    def valid(p):
        return (p >= 0) & (p < ndom)

    fetches = [
        pltpu.make_async_copy(source, target, in_sem.at[i])
        for i, (source, target) in enumerate((
            (state_hbm, state_ref), (send_hbm, send_ref),
            (owner_hbm, owner_ref), (neighbor_hbm, neighbor_ref),
            (volume_hbm, volume_ref), (normal_hbm, normal_ref),
            (oarm_hbm, oarm_ref), (narm_hbm, narm_ref),
            (step_hbm, step_ref), (table_hbm, table_ref),
        ))
    ]
    for fetch in fetches:
        fetch.start()
    gv_ref[...] = jnp.zeros(gv_ref.shape, F32)
    gg_ref[...] = jnp.zeros(gg_ref.shape, F32)

    barrier = pltpu.get_barrier_semaphore()
    for off in PEER_OFFSETS:
        @pl.when(valid(me + off))
        def _(off=off):
            pl.semaphore_signal(barrier, inc=1, device_id={"dom": me + off}, device_id_type=MESH)
    for k in range(1, ninst):
        pl.semaphore_signal(
            barrier, inc=1, device_id={"inst": lax.rem(mi + k, ninst)}, device_id_type=MESH
        )

    def ghost_copy(pay, dst, send, recv, sec, k, partition):
        return pltpu.make_async_remote_copy(
            src_ref=pay.at[sec, k],
            dst_ref=dst.at[sec, k],
            send_sem=send.at[sec, k],
            recv_sem=recv.at[sec, k],
            device_id={"dom": partition},
            device_id_type=MESH,
        )

    def ghosts_start(args, sec):
        for k, off in enumerate(PEER_OFFSETS):
            @pl.when(valid(me - off))
            def _(k=k, off=off):
                ghost_copy(*args, sec, k, me - off).start()

    def ghosts_wait(args, sec):
        for k, off in enumerate(PEER_OFFSETS):
            @pl.when(valid(me + off))
            def _(k=k, off=off):
                ghost_copy(*args, sec, k, me + off).wait_recv()

    def ghosts_sent(args, sec):
        for k, off in enumerate(PEER_OFFSETS):
            @pl.when(valid(me - off))
            def _(k=k, off=off):
                ghost_copy(*args, sec, k, me - off).wait_send()

    def peer_copy(sec, k):
        return pltpu.make_async_remote_copy(
            src_ref=own_ref.at[sec],
            dst_ref=peer_ref.at[sec, k - 1],
            send_sem=sp_send.at[sec, k - 1],
            recv_sem=sp_recv.at[sec, k - 1],
            device_id={"inst": lax.rem(mi + ninst - k, ninst)},
            device_id_type=MESH,
        )

    vargs = (payv_ref, gv_ref, sv_send, sv_recv)
    gargs = (payg_ref, gg_ref, sg_send, sg_recv)

    for fetch in fetches[:2]:
        fetch.wait()
    cell_id = lax.broadcasted_iota(jnp.int32, (cells, slots), 0)
    for k in range(4):
        hit = cell_id == send_ref[k:k + 1, :]
        st_ref[:, k * slots:(k + 1) * slots] = jnp.where(hit, 1.0, 0.0).astype(BF)

    pad = rows - nvar * idev
    filler = [jnp.zeros((pad, cells), F32)] if pad else []
    current = jnp.concatenate([state_ref[v] for v in range(nvar)] + filler, axis=0)
    own_ref[0] = current
    split = parts(current)

    def fill_payload(pay, sec, values):
        high = pay.shape[2]
        first = lax.broadcasted_iota(jnp.int32, (high, 2 * slots), 1) < slots
        for j in range(2):
            pair = values[:, j * 2 * slots:(j + 1) * 2 * slots]
            top, bottom = pair[:high], pair[pair.shape[0] - high:]
            pay[sec, 2 * j] = jnp.where(first, top, pltpu.roll(bottom, slots, 1))
            pay[sec, 2 * j + 1] = jnp.where(first, pltpu.roll(top, slots, 1), bottom)

    fill_payload(payv_ref, 0, joined(mm(split, st_ref[...])))

    neighbours = sum(valid(me + off).astype(jnp.int32) for off in PEER_OFFSETS)
    pl.semaphore_wait(barrier, neighbours + (ninst - 1))

    ghosts_start(vargs, 0)
    for k in range(1, ninst):
        peer_copy(0, k).start()

    for fetch in fetches[2:]:
        fetch.wait()
    def build(c, carry):
        at = pl.ds(pl.multiple_of(c * chunk, chunk), chunk)
        ids = lax.broadcasted_iota(jnp.int16, (cells + ghosts, chunk), 0)
        one, zero = jnp.ones((), BF), jnp.zeros((), BF)
        own = owner_ref[:, at].astype(jnp.int16)
        nbr = neighbor_ref[:, at].astype(jnp.int16)
        ot_ref[c] = jnp.where(ids[:cells] == own, one, zero)
        nt_ref[c] = jnp.where(ids == nbr, one, zero)
        return carry

    def build_sum(c, carry):
        pm_ref[c] = jnp.transpose(ot_ref[c] + nt_ref[c, :cells])
        return carry

    def build_difference(c, carry):
        dm_ref[c] = jnp.transpose(ot_ref[c] - nt_ref[c, :cells])
        return carry

    lax.fori_loop(0, chunks, build, 0)

    inv_volume = 1.0 / volume_ref[...]
    lane = lax.broadcasted_iota(jnp.int32, (1, chunk), 1)
    half = chunk // 2
    low_rows = lax.broadcasted_iota(jnp.int32, (2 * idev, half), 0) < idev

    def packed(x, v):
        tile = x[(v // 2) * 2 * idev:(v // 2 + 1) * 2 * idev]
        a, b = tile[:, :half], tile[:, half:]
        if v % 2 == 0:
            return jnp.where(low_rows, a, pltpu.roll(b, idev, 0))
        return jnp.where(low_rows, pltpu.roll(a, idev, 0), b)

    def unpacked(even, odd):
        if odd is None:
            a = jnp.where(low_rows, even, 0.0)
            b = jnp.where(low_rows, pltpu.roll(even, idev, 0), 0.0)
        else:
            a = jnp.where(low_rows, even, pltpu.roll(odd, idev, 0))
            b = jnp.where(low_rows, pltpu.roll(even, idev, 0), odd)
        return jnp.concatenate([a, b], axis=1)

    def both_halves(x):
        return jnp.where(low_rows, x[:, :half], x[:, half:])

    def ghost_values(ref, sec, wide):
        high = ref.shape[2]
        first = lax.broadcasted_iota(jnp.int32, (high, 2 * slots), 1) < slots
        pairs = []
        for j in range(2):
            a, b = ref[sec, 2 * j], ref[sec, 2 * j + 1]
            top = jnp.where(first, a, pltpu.roll(b, slots, 1))
            bottom = jnp.where(first, pltpu.roll(a, slots, 1), b)
            pairs.append(jnp.concatenate([top, bottom[2 * high - wide:]], axis=0))
        return jnp.concatenate(pairs, axis=1)

    def section(sec, split):
        def gather_local(c, carry):
            left_ref[c] = joined(mm(split, ot_ref[c]))
            right_ref[c] = joined(mm(split, nt_ref[c, :cells]))
            return carry

        lax.fori_loop(0, chunks, gather_local, 0)
        if sec == 0:
            lax.fori_loop(0, chunks, build_sum, 0)
        ghosts_wait(vargs, sec)
        gsplit = parts(ghost_values(gv_ref, sec, rows))
        acc_ref[...] = jnp.zeros(acc_ref.shape, F32)

        def gradient_step(c, carry):
            at = pl.ds(pl.multiple_of(c * chunk, chunk), chunk)
            right = right_ref[c] + joined(mm(gsplit, nt_ref[c, cells:]))
            right_ref[c] = right
            live = (lane + c * chunk) < count_ref[0]
            jump = jnp.where(live, 0.5 * (right - left_ref[c]), 0.0)
            flow = jnp.concatenate([jump * normal_ref[d:d + 1, at] for d in range(3)], axis=0)
            acc_ref[...] += joined(mm(parts(flow), pm_ref[c]))
            return carry

        lax.fori_loop(0, chunks, gradient_step, 0)
        gradient = acc_ref[...] * inv_volume
        dsplit = parts(gradient)
        fill_payload(payg_ref, sec, joined(mm(dsplit, st_ref[...])))
        ghosts_start(gargs, sec)

        def reconstruct(c, carry):
            at = pl.ds(pl.multiple_of(c * chunk, chunk), chunk)
            left = joined(mm(dsplit, ot_ref[c]))
            right = joined(mm(dsplit, nt_ref[c, :cells]))
            tl, tr = left_ref[c], right_ref[c]
            for d in range(3):
                tl = tl + left[d * rows:(d + 1) * rows] * oarm_ref[d:d + 1, at]
                tr = tr + right[d * rows:(d + 1) * rows] * narm_ref[d:d + 1, at]
            left_ref[c] = tl
            right_ref[c] = tr
            return carry

        lax.fori_loop(0, chunks, reconstruct, 0)
        if sec == 0:
            lax.fori_loop(0, chunks, build_difference, 0)

        for k in range(1, ninst):
            peer_copy(sec, k).wait_recv()
        every = jnp.concatenate(
            [own_ref[sec]] + [peer_ref[sec, k - 1] for k in range(1, ninst)], axis=0
        )
        high = every.astype(BF).astype(F32)
        stacked = jnp.concatenate([every, every - high, every], axis=0).astype(BF)
        spectral = mm(table_ref[...], stacked)

        ghosts_wait(gargs, sec)
        hsplit = parts(ghost_values(gg_ref, sec, 3 * rows))
        acc_ref[:rows] = jnp.zeros((rows, cells), F32)

        def flux_step(c, carry):
            at = pl.ds(pl.multiple_of(c * chunk, chunk), chunk)
            extra = joined(mm(hsplit, nt_ref[c, cells:]))
            tl, tr = left_ref[c], right_ref[c]
            for d in range(3):
                tr = tr + extra[d * rows:(d + 1) * rows] * narm_ref[d:d + 1, at]
            normals = [both_halves(normal_ref[d:d + 1, at]) for d in range(3)]
            area = jnp.sqrt(
                normals[0] * normals[0] + normals[1] * normals[1] + normals[2] * normals[2]
            )
            ul = [packed(tl, v) for v in range(nvar)]
            ur = [packed(tr, v) for v in range(nvar)]
            fl, sl = euler_flux(ul, normals, area)
            fr, sr = euler_flux(ur, normals, area)
            wave = jnp.maximum(sl, sr)
            flux = [
                0.5 * ((fl[v] + fr[v]) - wave * (ur[v] - ul[v])) for v in range(nvar)
            ] + [None]
            face = jnp.concatenate(
                [unpacked(flux[2 * j], flux[2 * j + 1]) for j in range((nvar + 1) // 2)], axis=0
            )
            live = (lane + c * chunk) < count_ref[0]
            face = jnp.where(live, face, 0.0)
            acc_ref[:rows] += joined(mm(parts(face), dm_ref[c]))
            return carry

        lax.fori_loop(0, chunks, flux_step, 0)
        return acc_ref[:rows] * inv_volume + FREQUENCY * spectral

    step = step_ref[...]
    current = current - 0.5 * step * section(0, split)
    own_ref[1] = current
    split = parts(current)
    fill_payload(payv_ref, 1, joined(mm(split, st_ref[...])))
    ghosts_start(vargs, 1)
    for k in range(1, ninst):
        peer_copy(1, k).start()
    residual = section(1, split)
    new = own_ref[0] - step * residual
    for v in range(nvar):
        new_ref[v] = new[v * idev:(v + 1) * idev]
        res_ref[v] = residual[v * idev:(v + 1) * idev]

    for sec in range(2):
        ghosts_sent(vargs, sec)
        ghosts_sent(gargs, sec)
        for k in range(1, ninst):
            peer_copy(sec, k).wait_send()


def solution(mesh):
    ndom, ninst = mesh.shape["dom"], mesh.shape["inst"]

    def local(
        state, cell_volume, step_size, face_normal, owner_arm, neighbor_arm,
        face_owner, face_neighbor, face_count, send_cells,
    ):
        nvar, idev, cells = state.shape
        faces = face_owner.shape[0]
        slots = send_cells.shape[1]
        chunk = min(2048, faces)
        chunks = faces // chunk
        rows = -(-nvar * idev // 8) * 8
        ghosts = 4 * slots
        vhigh = -(-rows // 16) * 8
        ghigh = -(-3 * rows // 16) * 8
        dims = (ndom, ninst, nvar, idev, cells, slots, chunks, chunk, rows)
        table = jnp.asarray(spectral_matrix(idev * ninst, idev, nvar, rows))
        vmem = pl.BlockSpec(memory_space=pltpu.VMEM)
        hbm = pl.BlockSpec(memory_space=pltpu.HBM)
        shape = jax.ShapeDtypeStruct(state.shape, F32)
        dma = pltpu.SemaphoreType.DMA
        return pl.pallas_call(
            functools.partial(kernel, dims),
            out_shape=(shape, shape),
            in_specs=[hbm] * 8 + [pl.BlockSpec(memory_space=pltpu.SMEM)] + [hbm] * 2,
            out_specs=(vmem, vmem),
            scratch_shapes=[
                pltpu.VMEM(state.shape, F32),
                pltpu.VMEM((1, cells), F32),
                pltpu.VMEM((1, cells), F32),
                pltpu.VMEM((3, faces), F32),
                pltpu.VMEM((3, faces), F32),
                pltpu.VMEM((3, faces), F32),
                pltpu.VMEM((1, faces), jnp.int32),
                pltpu.VMEM((1, faces), jnp.int32),
                pltpu.VMEM((4, slots), jnp.int32),
                pltpu.VMEM(table.shape, BF),
                dma((10,)),
                pltpu.VMEM((2, rows, cells), F32),
                pltpu.VMEM((2, ninst - 1, rows, cells), F32),
                pltpu.VMEM((2, 4, vhigh, 2 * slots), F32),
                pltpu.VMEM((2, 4, ghigh, 2 * slots), F32),
                pltpu.VMEM((2, 4, vhigh, 2 * slots), F32),
                pltpu.VMEM((2, 4, ghigh, 2 * slots), F32),
                pltpu.VMEM((cells, ghosts), BF),
                pltpu.VMEM((chunks, cells, chunk), BF),
                pltpu.VMEM((chunks, cells + ghosts, chunk), BF),
                pltpu.VMEM((chunks, chunk, cells), BF),
                pltpu.VMEM((chunks, chunk, cells), BF),
                pltpu.VMEM((chunks, rows, chunk), F32),
                pltpu.VMEM((chunks, rows, chunk), F32),
                pltpu.VMEM((3 * rows, cells), F32),
                dma((2, 4)), dma((2, 4)), dma((2, 4)), dma((2, 4)),
                dma((2, ninst - 1)), dma((2, ninst - 1)),
            ],
            compiler_params=pltpu.CompilerParams(
                collective_id=0, has_side_effects=True, vmem_limit_bytes=40 * 1024 * 1024
            ),
        )(*[
            x if x.size == 1 else pltpu.with_memory_space_constraint(x, pltpu.HBM)
            for x in (
                state, cell_volume[None], step_size[None], face_normal, owner_arm, neighbor_arm,
                face_owner[None], face_neighbor[None], face_count, send_cells, table,
            )
        ])

    placed = (
        P(None, "inst", "dom"),
        P("dom"),
        P("dom"),
        P(None, "dom"),
        P(None, "dom"),
        P(None, "dom"),
        P("dom"),
        P("dom"),
        P("dom"),
        P("dom", None),
    )
    return jax.shard_map(
        local,
        mesh=mesh,
        in_specs=placed,
        out_specs=(P(None, "inst", "dom"), P(None, "inst", "dom")),
        check_vma=False,
    )
```

```python
import functools

import jax
import jax.numpy as jnp
import numpy as np
from jax import lax
from jax.experimental import pallas as pl
from jax.experimental.pallas import tpu as pltpu
from jax.sharding import PartitionSpec as P

HEAT_RATIO = 1.4
FREQUENCY = 0.5
PEER_OFFSETS = (-2, -1, 1, 2)
MESH = pl.DeviceIdType.MESH
BF = jnp.bfloat16
F32 = jnp.float32


def spectral_matrix(points, inst_dev, nvar, rows):
    peers = points // inst_dev
    table = np.zeros((rows, peers * rows))
    for k in range(peers):
        for v in range(nvar):
            for t in range(inst_dev):
                for j in range(inst_dev):
                    d = (t - j - k * inst_dev) % points
                    if d:
                        table[v * inst_dev + t, k * rows + v * inst_dev + j] = (
                            0.5 * (-1.0) ** d / np.tan(np.pi * d / points)
                        )
    table = table.astype(np.float32)
    high = table.astype(jnp.bfloat16).astype(np.float32)
    low = table - high
    return np.concatenate([high, high, low], axis=1).astype(jnp.bfloat16)


def parts(x):
    high = x.astype(BF).astype(F32)
    return jnp.concatenate([x, x - high], axis=0).astype(BF)


def joined(y):
    half = y.shape[0] // 2
    return y[:half] + y[half:]


def mm(a, b):
    return lax.dot_general(a, b, (((1,), (0,)), ((), ())), preferred_element_type=F32)


def euler_flux(u, n, area):
    rho, m1, m2, m3, energy = u
    inv = 1.0 / rho
    u1, u2, u3 = m1 * inv, m2 * inv, m3 * inv
    pressure = (HEAT_RATIO - 1.0) * (energy - 0.5 * (m1 * u1 + m2 * u2 + m3 * u3))
    q = u1 * n[0] + u2 * n[1] + u3 * n[2]
    flux = (
        rho * q,
        m1 * q + pressure * n[0],
        m2 * q + pressure * n[1],
        m3 * q + pressure * n[2],
        (energy + pressure) * q,
    )
    speed = jnp.abs(q) + jnp.sqrt(HEAT_RATIO * pressure * inv) * area
    return flux, speed


def kernel(
    dims,
    state_hbm, volume_hbm, step_hbm, normal_hbm, oarm_hbm, narm_hbm, owner_hbm, neighbor_hbm,
    count_ref, send_hbm, table_hbm,
    new_ref, res_ref,
    state_ref, volume_ref, step_ref, normal_ref, oarm_ref, narm_ref, owner_ref, neighbor_ref,
    send_ref, table_ref, in_sem,
    own_ref, peer_ref, payv_ref, payg_ref, gv_ref, gg_ref,
    st_ref, ot_ref, nt_ref, pm_ref, dm_ref, left_ref, right_ref, acc_ref,
    sv_send, sv_recv, sg_send, sg_recv, sp_send, sp_recv,
):
    ndom, ninst, nvar, idev, cells, slots, chunks, chunk, rows = dims
    ghosts = 4 * slots
    me = lax.axis_index("dom")
    mi = lax.axis_index("inst")

    def valid(p):
        return (p >= 0) & (p < ndom)

    fetches = [
        pltpu.make_async_copy(source, target, in_sem.at[i])
        for i, (source, target) in enumerate((
            (state_hbm, state_ref), (send_hbm, send_ref),
            (owner_hbm, owner_ref), (neighbor_hbm, neighbor_ref),
            (volume_hbm, volume_ref), (normal_hbm, normal_ref),
            (oarm_hbm, oarm_ref), (narm_hbm, narm_ref),
            (step_hbm, step_ref), (table_hbm, table_ref),
        ))
    ]
    for fetch in fetches:
        fetch.start()
    gv_ref[...] = jnp.zeros(gv_ref.shape, F32)
    gg_ref[...] = jnp.zeros(gg_ref.shape, F32)

    barrier = pltpu.get_barrier_semaphore()
    for off in PEER_OFFSETS:
        @pl.when(valid(me + off))
        def _(off=off):
            pl.semaphore_signal(barrier, inc=1, device_id={"dom": me + off}, device_id_type=MESH)
    for k in range(1, ninst):
        pl.semaphore_signal(
            barrier, inc=1, device_id={"inst": lax.rem(mi + k, ninst)}, device_id_type=MESH
        )

    def ghost_copy(pay, dst, send, recv, sec, k, partition):
        return pltpu.make_async_remote_copy(
            src_ref=pay.at[sec, k],
            dst_ref=dst.at[sec, k],
            send_sem=send.at[sec, k],
            recv_sem=recv.at[sec, k],
            device_id={"dom": partition},
            device_id_type=MESH,
        )

    def ghosts_start(args, sec):
        for k, off in enumerate(PEER_OFFSETS):
            @pl.when(valid(me - off))
            def _(k=k, off=off):
                ghost_copy(*args, sec, k, me - off).start()

    def ghosts_wait(args, sec):
        for k, off in enumerate(PEER_OFFSETS):
            @pl.when(valid(me + off))
            def _(k=k, off=off):
                ghost_copy(*args, sec, k, me + off).wait_recv()

    def ghosts_sent(args, sec):
        for k, off in enumerate(PEER_OFFSETS):
            @pl.when(valid(me - off))
            def _(k=k, off=off):
                ghost_copy(*args, sec, k, me - off).wait_send()

    def peer_copy(sec, k):
        return pltpu.make_async_remote_copy(
            src_ref=own_ref.at[sec],
            dst_ref=peer_ref.at[sec, k - 1],
            send_sem=sp_send.at[sec, k - 1],
            recv_sem=sp_recv.at[sec, k - 1],
            device_id={"inst": lax.rem(mi + ninst - k, ninst)},
            device_id_type=MESH,
        )

    vargs = (payv_ref, gv_ref, sv_send, sv_recv)
    gargs = (payg_ref, gg_ref, sg_send, sg_recv)

    for fetch in fetches[:2]:
        fetch.wait()
    cell_id = lax.broadcasted_iota(jnp.int32, (cells, slots), 0)
    for k in range(4):
        hit = cell_id == send_ref[k:k + 1, :]
        st_ref[:, k * slots:(k + 1) * slots] = jnp.where(hit, 1.0, 0.0).astype(BF)

    pad = rows - nvar * idev
    filler = [jnp.zeros((pad, cells), F32)] if pad else []
    current = jnp.concatenate([state_ref[v] for v in range(nvar)] + filler, axis=0)
    own_ref[0] = current
    split = parts(current)

    def fill_payload(pay, sec, values):
        high = pay.shape[2]
        first = lax.broadcasted_iota(jnp.int32, (high, 2 * slots), 1) < slots
        for j in range(2):
            pair = values[:, j * 2 * slots:(j + 1) * 2 * slots]
            top, bottom = pair[:high], pair[pair.shape[0] - high:]
            pay[sec, 2 * j] = jnp.where(first, top, pltpu.roll(bottom, slots, 1))
            pay[sec, 2 * j + 1] = jnp.where(first, pltpu.roll(top, slots, 1), bottom)

    fill_payload(payv_ref, 0, joined(mm(split, st_ref[...])))

    neighbours = sum(valid(me + off).astype(jnp.int32) for off in PEER_OFFSETS)
    pl.semaphore_wait(barrier, neighbours + (ninst - 1))

    ghosts_start(vargs, 0)
    for k in range(1, ninst):
        peer_copy(0, k).start()

    for fetch in fetches[2:]:
        fetch.wait()
    def build(c, carry):
        at = pl.ds(pl.multiple_of(c * chunk, chunk), chunk)
        ids = lax.broadcasted_iota(jnp.int16, (cells + ghosts, chunk), 0)
        one, zero = jnp.ones((), BF), jnp.zeros((), BF)
        own = owner_ref[:, at].astype(jnp.int16)
        nbr = neighbor_ref[:, at].astype(jnp.int16)
        ot_ref[c] = jnp.where(ids[:cells] == own, one, zero)
        nt_ref[c] = jnp.where(ids == nbr, one, zero)
        return carry

    def build_sum(c, carry):
        pm_ref[c] = jnp.transpose(ot_ref[c] + nt_ref[c, :cells])
        return carry

    def build_difference(c, carry):
        dm_ref[c] = jnp.transpose(ot_ref[c] - nt_ref[c, :cells])
        return carry

    lax.fori_loop(0, chunks, build, 0, unroll=True)

    inv_volume = 1.0 / volume_ref[...]
    lane = lax.broadcasted_iota(jnp.int32, (1, chunk), 1)
    half = chunk // 2
    low_rows = lax.broadcasted_iota(jnp.int32, (2 * idev, half), 0) < idev

    def packed(x, v):
        tile = x[(v // 2) * 2 * idev:(v // 2 + 1) * 2 * idev]
        a, b = tile[:, :half], tile[:, half:]
        if v % 2 == 0:
            return jnp.where(low_rows, a, pltpu.roll(b, idev, 0))
        return jnp.where(low_rows, pltpu.roll(a, idev, 0), b)

    def unpacked(even, odd):
        if odd is None:
            a = jnp.where(low_rows, even, 0.0)
            b = jnp.where(low_rows, pltpu.roll(even, idev, 0), 0.0)
        else:
            a = jnp.where(low_rows, even, pltpu.roll(odd, idev, 0))
            b = jnp.where(low_rows, pltpu.roll(even, idev, 0), odd)
        return jnp.concatenate([a, b], axis=1)

    def both_halves(x):
        return jnp.where(low_rows, x[:, :half], x[:, half:])

    def ghost_values(ref, sec, wide):
        high = ref.shape[2]
        first = lax.broadcasted_iota(jnp.int32, (high, 2 * slots), 1) < slots
        pairs = []
        for j in range(2):
            a, b = ref[sec, 2 * j], ref[sec, 2 * j + 1]
            top = jnp.where(first, a, pltpu.roll(b, slots, 1))
            bottom = jnp.where(first, pltpu.roll(a, slots, 1), b)
            pairs.append(jnp.concatenate([top, bottom[2 * high - wide:]], axis=0))
        return jnp.concatenate(pairs, axis=1)

    def section(sec, split):
        def gather_local(c, carry):
            left_ref[c] = joined(mm(split, ot_ref[c]))
            right_ref[c] = joined(mm(split, nt_ref[c, :cells]))
            return carry

        lax.fori_loop(0, chunks, gather_local, 0, unroll=True)
        if sec == 0:
            lax.fori_loop(0, chunks, build_sum, 0, unroll=True)
        ghosts_wait(vargs, sec)
        gsplit = parts(ghost_values(gv_ref, sec, rows))
        acc_ref[...] = jnp.zeros(acc_ref.shape, F32)

        def gradient_step(c, carry):
            at = pl.ds(pl.multiple_of(c * chunk, chunk), chunk)
            right = right_ref[c] + joined(mm(gsplit, nt_ref[c, cells:]))
            right_ref[c] = right
            live = (lane + c * chunk) < count_ref[0]
            jump = jnp.where(live, 0.5 * (right - left_ref[c]), 0.0)
            flow = jnp.concatenate([jump * normal_ref[d:d + 1, at] for d in range(3)], axis=0)
            acc_ref[...] += joined(mm(parts(flow), pm_ref[c]))
            return carry

        lax.fori_loop(0, chunks, gradient_step, 0, unroll=True)
        gradient = acc_ref[...] * inv_volume
        dsplit = parts(gradient)
        fill_payload(payg_ref, sec, joined(mm(dsplit, st_ref[...])))
        ghosts_start(gargs, sec)

        def reconstruct(c, carry):
            at = pl.ds(pl.multiple_of(c * chunk, chunk), chunk)
            left = joined(mm(dsplit, ot_ref[c]))
            right = joined(mm(dsplit, nt_ref[c, :cells]))
            tl, tr = left_ref[c], right_ref[c]
            for d in range(3):
                tl = tl + left[d * rows:(d + 1) * rows] * oarm_ref[d:d + 1, at]
                tr = tr + right[d * rows:(d + 1) * rows] * narm_ref[d:d + 1, at]
            left_ref[c] = tl
            right_ref[c] = tr
            return carry

        lax.fori_loop(0, chunks, reconstruct, 0, unroll=True)
        if sec == 0:
            lax.fori_loop(0, chunks, build_difference, 0, unroll=True)

        for k in range(1, ninst):
            peer_copy(sec, k).wait_recv()
        every = jnp.concatenate(
            [own_ref[sec]] + [peer_ref[sec, k - 1] for k in range(1, ninst)], axis=0
        )
        high = every.astype(BF).astype(F32)
        stacked = jnp.concatenate([every, every - high, every], axis=0).astype(BF)
        spectral = mm(table_ref[...], stacked)

        ghosts_wait(gargs, sec)
        hsplit = parts(ghost_values(gg_ref, sec, 3 * rows))
        acc_ref[:rows] = jnp.zeros((rows, cells), F32)

        def flux_step(c, carry):
            at = pl.ds(pl.multiple_of(c * chunk, chunk), chunk)
            extra = joined(mm(hsplit, nt_ref[c, cells:]))
            tl, tr = left_ref[c], right_ref[c]
            for d in range(3):
                tr = tr + extra[d * rows:(d + 1) * rows] * narm_ref[d:d + 1, at]
            normals = [both_halves(normal_ref[d:d + 1, at]) for d in range(3)]
            area = jnp.sqrt(
                normals[0] * normals[0] + normals[1] * normals[1] + normals[2] * normals[2]
            )
            ul = [packed(tl, v) for v in range(nvar)]
            ur = [packed(tr, v) for v in range(nvar)]
            fl, sl = euler_flux(ul, normals, area)
            fr, sr = euler_flux(ur, normals, area)
            wave = jnp.maximum(sl, sr)
            flux = [
                0.5 * ((fl[v] + fr[v]) - wave * (ur[v] - ul[v])) for v in range(nvar)
            ] + [None]
            face = jnp.concatenate(
                [unpacked(flux[2 * j], flux[2 * j + 1]) for j in range((nvar + 1) // 2)], axis=0
            )
            live = (lane + c * chunk) < count_ref[0]
            face = jnp.where(live, face, 0.0)
            acc_ref[:rows] += joined(mm(parts(face), dm_ref[c]))
            return carry

        lax.fori_loop(0, chunks, flux_step, 0, unroll=True)
        return acc_ref[:rows] * inv_volume + FREQUENCY * spectral

    step = step_ref[...]
    current = current - 0.5 * step * section(0, split)
    own_ref[1] = current
    split = parts(current)
    fill_payload(payv_ref, 1, joined(mm(split, st_ref[...])))
    ghosts_start(vargs, 1)
    for k in range(1, ninst):
        peer_copy(1, k).start()
    residual = section(1, split)
    new = own_ref[0] - step * residual
    for v in range(nvar):
        new_ref[v] = new[v * idev:(v + 1) * idev]
        res_ref[v] = residual[v * idev:(v + 1) * idev]

    for sec in range(2):
        ghosts_sent(vargs, sec)
        ghosts_sent(gargs, sec)
        for k in range(1, ninst):
            peer_copy(sec, k).wait_send()


def solution(mesh):
    ndom, ninst = mesh.shape["dom"], mesh.shape["inst"]

    def local(
        state, cell_volume, step_size, face_normal, owner_arm, neighbor_arm,
        face_owner, face_neighbor, face_count, send_cells,
    ):
        nvar, idev, cells = state.shape
        faces = face_owner.shape[0]
        slots = send_cells.shape[1]
        chunk = min(512, faces)
        chunks = faces // chunk
        rows = -(-nvar * idev // 8) * 8
        ghosts = 4 * slots
        vhigh = -(-rows // 16) * 8
        ghigh = -(-3 * rows // 16) * 8
        dims = (ndom, ninst, nvar, idev, cells, slots, chunks, chunk, rows)
        table = jnp.asarray(spectral_matrix(idev * ninst, idev, nvar, rows))
        vmem = pl.BlockSpec(memory_space=pltpu.VMEM)
        hbm = pl.BlockSpec(memory_space=pltpu.HBM)
        shape = jax.ShapeDtypeStruct(state.shape, F32)
        dma = pltpu.SemaphoreType.DMA
        return pl.pallas_call(
            functools.partial(kernel, dims),
            out_shape=(shape, shape),
            in_specs=[hbm] * 8 + [pl.BlockSpec(memory_space=pltpu.SMEM)] + [hbm] * 2,
            out_specs=(vmem, vmem),
            scratch_shapes=[
                pltpu.VMEM(state.shape, F32),
                pltpu.VMEM((1, cells), F32),
                pltpu.VMEM((1, cells), F32),
                pltpu.VMEM((3, faces), F32),
                pltpu.VMEM((3, faces), F32),
                pltpu.VMEM((3, faces), F32),
                pltpu.VMEM((1, faces), jnp.int32),
                pltpu.VMEM((1, faces), jnp.int32),
                pltpu.VMEM((4, slots), jnp.int32),
                pltpu.VMEM(table.shape, BF),
                dma((10,)),
                pltpu.VMEM((2, rows, cells), F32),
                pltpu.VMEM((2, ninst - 1, rows, cells), F32),
                pltpu.VMEM((2, 4, vhigh, 2 * slots), F32),
                pltpu.VMEM((2, 4, ghigh, 2 * slots), F32),
                pltpu.VMEM((2, 4, vhigh, 2 * slots), F32),
                pltpu.VMEM((2, 4, ghigh, 2 * slots), F32),
                pltpu.VMEM((cells, ghosts), BF),
                pltpu.VMEM((chunks, cells, chunk), BF),
                pltpu.VMEM((chunks, cells + ghosts, chunk), BF),
                pltpu.VMEM((chunks, chunk, cells), BF),
                pltpu.VMEM((chunks, chunk, cells), BF),
                pltpu.VMEM((chunks, rows, chunk), F32),
                pltpu.VMEM((chunks, rows, chunk), F32),
                pltpu.VMEM((3 * rows, cells), F32),
                dma((2, 4)), dma((2, 4)), dma((2, 4)), dma((2, 4)),
                dma((2, ninst - 1)), dma((2, ninst - 1)),
            ],
            compiler_params=pltpu.CompilerParams(
                collective_id=0, has_side_effects=True, vmem_limit_bytes=40 * 1024 * 1024
            ),
        )(*[
            x if x.size == 1 else pltpu.with_memory_space_constraint(x, pltpu.HBM)
            for x in (
                state, cell_volume[None], step_size[None], face_normal, owner_arm, neighbor_arm,
                face_owner[None], face_neighbor[None], face_count, send_cells, table,
            )
        ])

    placed = (
        P(None, "inst", "dom"),
        P("dom"),
        P("dom"),
        P(None, "dom"),
        P(None, "dom"),
        P(None, "dom"),
        P("dom"),
        P("dom"),
        P("dom"),
        P("dom", None),
    )
    return jax.shard_map(
        local,
        mesh=mesh,
        in_specs=placed,
        out_specs=(P(None, "inst", "dom"), P(None, "inst", "dom")),
        check_vma=False,
    )
```
